32 devices in a mesh: area: 4 (over z), line: 8 (over y, x, core).
Axes of the slice: x: 2, y: 2, z: 4, core: 2. Of those that a mesh axis runs over, the one named last changes fastest.
Arguments:
- traces: bfloat16 [8192, 2048], P(('area', 'line')), may hold values from -6 to 6
- owner: int32 [8192, 1], P(('area', 'line')), may hold values from 0 to 7; in each aligned block of 256 rows (0 to 255, 256 to 511, ...) at most 64 rows name the same one
- panel_index: int32 [8192], P(('area', 'line')), may hold values from 0 to 319
- receiver_slot: int32 [8192], P(('area', 'line')), may hold values from 0 to 63
- aperture_weight: float32 [8192], P(('area', 'line')), may hold values from 0.5 to 1.5
- panels: bfloat16 [4, 8, 256, 2048], P('area', 'line'), may hold values from -6 to 6
- plan: int32 [4, 4], replicated, may hold values from 0 to 7
Outputs:
- multiples: bfloat16 [4, 2048, 2048], P(None, ('area', 'line'))
The draws below stay inside these ranges and needn't reach their ends.
Inputs may be any that keep to these rules, and one draw needn't show every extreme that they name: Among the traces of one device, no owner is named by more than 64 traces; some owner is named by exactly 64 of them.
All inputs are finite; a program needn't handle non-finite values.
Results may differ from the reference program's by a relative error of at most 0.014.
Values may be sent and summed in bfloat16 or wider, within the bound.
No kernel may reach another device: no remote copies, remote signals or barrier semaphores. Data moves between devices by JAX's collectives and lax.ppermute only.
A program may use at most 128 MiB of HBM per device.

```python
import math
import jax
import jax.numpy as jnp
import numpy as np

NT = 2048
NF = 1024
PANEL = 256
EDGE = 64
STEPS = 4
ROWS_DEV = 256
RECV_DEV = 64
LINES = 8
AREAS = 4
CAP = 64
TRACES = 8192


def plant(array, key, low, high):
    longest = array.shape.index(max(array.shape))
    spots = []
    for shift in (0, 1):
        where = [jax.random.randint(jax.random.fold_in(key, axis), (), 0, length) for axis, length in enumerate(array.shape)]
        where[longest] = (where[longest] + shift) % array.shape[longest]
        spots.append(tuple(where))
    return array.at[spots[0]].set(low).at[spots[1]].set(high)


def steps_of(own_key, extent, shards, least, top_value):
    factor_of, own = 1.0, jax.random.fold_in(own_key, 6)
    for position, shards_of in shards:
        heights = jnp.exp(jax.random.uniform(jax.random.fold_in(own, position), (shards_of,), jnp.float32, least / len(shards), top_value / len(shards)))
        factor_of = factor_of * jnp.repeat(heights, extent[position] // shards_of).reshape([-1 if axis == position else 1 for axis in range(len(extent))])
    return factor_of


def deal_out(rng, own, number, rows, count, top, bound, skew):
    order = jax.random.permutation(rng, count)
    heavy_load, usual = shares(count, rows * top, bound, skew, True), shares(count, rows * top, bound, skew, False)
    places = jnp.arange(count)

    def named(lengths, rotation):
        used = int((lengths > 0).sum())
        fixed = max(1, used // 4)
        passed = fixed + (places - fixed + rotation * (used - fixed)) % max(1, count - fixed)
        return jnp.zeros((count,), jnp.int32).at[order[jnp.where(places < fixed, places, passed)]].set(jnp.asarray(lengths, jnp.int32))

    lengths = jnp.where(number % 4 == 0, named(heavy_load, number // 4), named(usual, number - number // 4 - 1))
    mixed = jax.random.permutation(jax.random.fold_in(own, 3), count)
    donor, sink = mixed[0:count // 2 * 2:2], mixed[1:count // 2 * 2:2]
    room = jnp.minimum(lengths[donor] - 1, bound - lengths[sink]) // 2
    room = jnp.where((donor == order[0]) | (sink == order[0]) | (lengths[sink] == 0), 0, jnp.maximum(room, 0))
    passed = jax.random.randint(jax.random.fold_in(own, 4), (count // 2,), 0, 1 << 20) % (room + 1)
    lengths = lengths.at[donor].add(-passed).at[sink].add(passed)
    labels = jnp.searchsorted(jnp.cumsum(lengths), jnp.arange(rows * top), side="right").astype(jnp.int32)
    grid = labels.reshape(top, rows).T
    grid = grid[jax.random.permutation(jax.random.fold_in(own, 1), rows)]
    rotation = jax.random.randint(jax.random.fold_in(own, 2), (rows, 1), 0, top)
    return jnp.take_along_axis(grid, (jnp.arange(top)[None, :] + rotation) % top, axis=1)


def shares(count, total, limit, slope, full):
    loads = [(1 << 20) // math.isqrt(rank ** slope) + 1 for rank in range(1, count + 1)]
    largest = limit if full else min(limit, max(-(-total // count), total * loads[0] // sum(loads)))
    least = 1 if total - largest >= count - 1 else 0
    holding, spare = [largest] + [least] * (count - 1), total - largest - least * (count - 1)
    while spare > 0:
        candidates = [i for i in range(1, count) if holding[i] < largest] or [i for i in range(1, count) if holding[i] < limit]
        pool, remaining = sum([loads[i] for i in candidates]), spare
        for i in candidates:
            extra = min(limit - holding[i], max(1, remaining * loads[i] // pool), spare)
            holding[i] = holding[i] + extra
            spare = spare - extra
    return np.array(holding)


def scatter_about(own_key, shape, width, bound, pieces=(), kind=jnp.bfloat16):
    drawn = jax.random.normal(own_key, shape, jnp.float32) * width
    if len(pieces) > 0:
        drawn = steps_of(own_key, shape, pieces, -0.22, 0.18) * drawn
    return jnp.clip(drawn, min=-bound, max=bound).astype(kind)


def setup_inputs(seed: int = 0) -> dict:
    seeds = jax.random.split(jax.random.key(seed), 8)
    traces = scatter_about(seeds[0], (TRACES, NT), 1.0, 6.0, ((0, 32),))
    owner_keys = jax.random.split(jax.random.fold_in(seeds[1], 1), TRACES // ROWS_DEV)
    owner_turns = jax.random.permutation(jax.random.fold_in(seeds[1], 3), TRACES // ROWS_DEV)
    owner = jax.vmap(lambda own, number: deal_out(jax.random.fold_in(seeds[1], 2), own, number, ROWS_DEV, LINES, 1, CAP, 2))(owner_keys, owner_turns).reshape((TRACES, 1))
    panel_index = plant(jax.random.randint(seeds[2], (TRACES,), 0, PANEL + EDGE), jax.random.fold_in(seeds[2], 1), 0, (PANEL + EDGE) - 1).astype(jnp.int32)
    receiver_slot = plant(jax.random.randint(seeds[3], (TRACES,), 0, RECV_DEV), jax.random.fold_in(seeds[3], 1), 0, RECV_DEV - 1).astype(jnp.int32)
    aperture_weight = jnp.clip(0.5 + 1.0 * jax.random.uniform(seeds[4], (TRACES,), jnp.float32) ** steps_of(seeds[4], (TRACES,), ((0, 32),), -0.2, 0.2), 0.5, 1.5)
    panels = scatter_about(seeds[5], (AREAS, LINES, PANEL, NT), 1.0, 6.0, ((0, 4), (1, 8)))
    plan = plant(jax.random.randint(seeds[6], (AREAS, STEPS), 0, LINES), jax.random.fold_in(seeds[6], 1), 0, LINES - 1).astype(jnp.int32)
    return dict(traces=traces, owner=owner, panel_index=panel_index, receiver_slot=receiver_slot, aperture_weight=aperture_weight, panels=panels, plan=plan)


def make_tables(samples, bins):
    sample_ids = jnp.arange(samples, dtype=jnp.int32)
    bin_ids = jnp.arange(bins, dtype=jnp.int32)
    phases = (sample_ids[:, None] * bin_ids[None, :] % samples).astype(jnp.float32) * (2.0 * math.pi / samples)
    scaling = 1.0 / math.sqrt(samples)
    forward = (jnp.concatenate([jnp.cos(phases), -jnp.sin(phases)], 1) * scaling).astype(jnp.bfloat16)
    weights = jnp.where(bin_ids == 0, 1.0, 2.0).astype(jnp.float32)[:, None]
    inverse = (jnp.concatenate([jnp.cos(phases).T * weights, -jnp.sin(phases).T * weights], 0) * scaling).astype(jnp.bfloat16)
    return (forward, inverse)

def reference(traces, owner, panel_index, receiver_slot, aperture_weight, panels, plan):
    forward, inverse = make_tables(NT, NF)
    forward_wide = forward.astype(jnp.float32)
    inverse_wide = inverse.astype(jnp.float32)
    trace_spectra = jnp.dot(traces.astype(jnp.float32), forward_wide).astype(jnp.bfloat16)
    per_area = LINES * ROWS_DEV
    outputs = []
    for panel_step in range(STEPS):
        spectra_list = []
        for area_no in range(AREAS):
            chosen = panels[area_no, plan[area_no, panel_step]]
            spectra_list.append(jnp.dot(chosen.astype(jnp.float32), forward_wide).astype(jnp.bfloat16))
        area_blocks = []
        for area_no in range(AREAS):
            if area_no == 0:
                border = jnp.zeros((EDGE, 2 * NF), jnp.bfloat16)
            else:
                border = spectra_list[area_no - 1][PANEL - EDGE:]
            extended = jnp.concatenate([spectra_list[area_no], border], 0)
            lower = area_no * per_area
            local_spec = trace_spectra[lower:lower + per_area].astype(jnp.float32)
            picked = extended[panel_index[lower:lower + per_area]].astype(jnp.float32)
            weight_now = aperture_weight[lower:lower + per_area][:, None]
            real_p, imag_p = (picked[:, :NF], picked[:, NF:])
            real_d, imag_d = (local_spec[:, :NF], local_spec[:, NF:])
            product = jnp.concatenate([(real_p * real_d - imag_p * imag_d) * weight_now, (real_p * imag_d + imag_p * real_d) * weight_now], 1).astype(jnp.bfloat16)
            target = owner[lower:lower + per_area, 0] * RECV_DEV + receiver_slot[lower:lower + per_area]
            summed = jax.ops.segment_sum(product.astype(jnp.float32), target, num_segments=LINES * RECV_DEV)
            receiver_spectra = summed.astype(jnp.bfloat16)
            area_blocks.append(jnp.dot(receiver_spectra.astype(jnp.float32), inverse_wide).astype(jnp.bfloat16))
        outputs.append(jnp.concatenate(area_blocks, 0))
    return jnp.stack(outputs, 0)
```

```python
import functools
import math

import jax
import jax.numpy as jnp
import ml_dtypes
import numpy as np
from jax import lax
from jax.experimental import pallas as pl
from jax.experimental.pallas import tpu as pltpu
from jax.sharding import PartitionSpec as P

NF = 1024
EDGE = 64
STEPS = 4
RECV_DEV = 64
META = 16
ITEMS = 4
BASE = 64
F32 = jnp.float32
BF16 = jnp.bfloat16


def vmem():
    return pl.BlockSpec(memory_space=pltpu.VMEM)


def smem():
    return pl.BlockSpec(memory_space=pltpu.SMEM)


@functools.lru_cache(maxsize=None)
def make_tables(samples, bins, owners):
    ids = np.arange(samples)[:, None] * np.arange(bins)[None, :] % samples
    phases = ids * (2.0 * math.pi / samples)
    scaling = 1.0 / math.sqrt(samples)
    each = bins // owners

    def blocks(real, imag):
        both = np.stack([real.reshape(samples, owners, each), imag.reshape(samples, owners, each)], 2)
        return both.reshape(samples, owners, 2 * each)

    forward = blocks(np.cos(phases), -np.sin(phases)) * scaling
    doubled = np.where(np.arange(bins) == 0, 1.0, 2.0)[None, :] * scaling
    inverse = blocks(np.cos(phases) * doubled, -np.sin(phases) * doubled)
    forward = np.ascontiguousarray(forward.transpose(1, 0, 2)).astype(ml_dtypes.bfloat16)
    inverse = np.ascontiguousarray(inverse.transpose(1, 2, 0)).astype(ml_dtypes.bfloat16)
    return forward, inverse


def transform_kernel(x_ref, table_ref, out_ref):
    out_ref[0] = jnp.dot(x_ref[...], table_ref[0], preferred_element_type=F32).astype(BF16)


def transform_panel(panel, table):
    rows, samples = panel.shape
    owners, _, cols = table.shape
    return pl.pallas_call(
        transform_kernel,
        grid=(owners,),
        out_shape=jax.ShapeDtypeStruct((owners, rows, cols), BF16),
        in_specs=[
            pl.BlockSpec((rows, samples), lambda j: (0, 0)),
            pl.BlockSpec((1, samples, cols), lambda j: (j, 0, 0)),
        ],
        out_specs=pl.BlockSpec((1, rows, cols), lambda j: (j, 0, 0)),
        cost_estimate=pl.CostEstimate(
            flops=2 * rows * samples * cols * owners,
            bytes_accessed=2 * (samples * cols * owners + rows * samples * 2),
            transcendentals=0,
        ),
        compiler_params=pltpu.CompilerParams(vmem_limit_bytes=16 << 20),
        name="panel_dft",
    )(panel, table)


def traces_kernel(x_ref, weight_ref, meta_ref, table_ref, out_ref):
    rows = x_ref.shape[0]
    spectra = jnp.dot(x_ref[...], table_ref[0], preferred_element_type=F32)
    out_ref[0, :rows, :] = (spectra * weight_ref[...]).astype(BF16)
    out_ref[0, rows:, :] = meta_ref[...]


def transform_traces(traces, weight, meta, table):
    rows, samples = traces.shape
    owners, _, cols = table.shape
    return pl.pallas_call(
        traces_kernel,
        grid=(owners,),
        out_shape=jax.ShapeDtypeStruct((owners, rows + META, cols), BF16),
        in_specs=[
            pl.BlockSpec((rows, samples), lambda j: (0, 0)),
            pl.BlockSpec((rows, 1), lambda j: (0, 0)),
            pl.BlockSpec((META, cols), lambda j: (0, 0)),
            pl.BlockSpec((1, samples, cols), lambda j: (j, 0, 0)),
        ],
        out_specs=pl.BlockSpec((1, rows + META, cols), lambda j: (j, 0, 0)),
        cost_estimate=pl.CostEstimate(
            flops=2 * rows * samples * cols * owners,
            bytes_accessed=2 * (samples * cols * owners + rows * samples * 2),
            transcendentals=0,
        ),
        compiler_params=pltpu.CompilerParams(vmem_limit_bytes=16 << 20),
        name="trace_dft",
    )(traces, weight, meta, table)


def product_kernel(plan_ref, got_ref, panels_ref, border_ref, out_ref, gather_ref, summer_ref):
    owners, rows_meta, cols = got_ref.shape
    rows = rows_meta - META
    half = cols // 2
    panel_rows = panels_ref.shape[1]
    per_item = rows // cols
    receivers = summer_ref.shape[0]
    step = pl.program_id(0)

    @pl.when(step == 0)
    def _():
        square = (cols, cols)
        eye = (
            lax.broadcasted_iota(jnp.int32, square, 0) == lax.broadcasted_iota(jnp.int32, square, 1)
        ).astype(BF16)
        for src in range(owners):
            meta = got_ref[src, rows:, :]
            wide = meta.astype(F32)
            turned = lax.dot_general(eye, meta, (((1,), (1,)), ((), ())), preferred_element_type=F32)
            for part in range(per_item):
                at = src * rows + part * cols
                owner = wide[part : part + 1]
                slot = wide[per_item + part : per_item + part + 1]
                number = (owner * RECV_DEV + slot).astype(jnp.int32)
                ids = lax.broadcasted_iota(jnp.int32, (receivers, cols), 0)
                summer_ref[:, at : at + cols] = (ids == number).astype(BF16)
                high = turned[:, 2 * per_item + part : 2 * per_item + part + 1]
                low = turned[:, 3 * per_item + part : 3 * per_item + part + 1]
                index = (high * BASE + low).astype(jnp.int32)
                ids = lax.broadcasted_iota(jnp.int32, (cols, panel_rows + EDGE), 1)
                gather_ref[at : at + cols, :] = (ids == index).astype(BF16)

    extended = jnp.concatenate([panels_ref[plan_ref[step]], border_ref[step]], 0)
    total = jnp.zeros((receivers, cols), F32)
    for src in range(owners):
        at = src * rows
        picked = jnp.dot(gather_ref[at : at + rows, :], extended, preferred_element_type=F32)
        spectra = got_ref[src, :rows, :].astype(F32)
        real_p, imag_p = picked[:, :half], picked[:, half:]
        real_d, imag_d = spectra[:, :half], spectra[:, half:]
        product = jnp.concatenate(
            [real_p * real_d - imag_p * imag_d, real_p * imag_d + imag_p * real_d], 1
        ).astype(BF16)
        total += jnp.dot(summer_ref[:, at : at + rows], product, preferred_element_type=F32)
    result = total.astype(BF16)
    for owner in range(owners):
        out_ref[owner, 0] = result[owner * RECV_DEV : (owner + 1) * RECV_DEV]


def receivers_of(plan_row, got, panels, border):
    owners, rows_meta, cols = got.shape
    rows = rows_meta - META
    panel_rows = panels.shape[1]
    receivers = owners * RECV_DEV
    extent = panel_rows + EDGE
    return pl.pallas_call(
        product_kernel,
        grid=(STEPS,),
        out_shape=jax.ShapeDtypeStruct((owners, STEPS, RECV_DEV, cols), BF16),
        in_specs=[smem(), vmem(), vmem(), vmem()],
        out_specs=pl.BlockSpec((owners, 1, RECV_DEV, cols), lambda k: (0, k, 0, 0)),
        scratch_shapes=[
            pltpu.VMEM((owners * rows, extent), BF16),
            pltpu.VMEM((receivers, owners * rows), BF16),
        ],
        cost_estimate=pl.CostEstimate(
            flops=2 * STEPS * owners * rows * cols * (extent + receivers),
            bytes_accessed=2 * cols * owners * (rows + panel_rows + STEPS * RECV_DEV),
            transcendentals=0,
        ),
        compiler_params=pltpu.CompilerParams(vmem_limit_bytes=40 << 20),
        name="receiver_sums",
    )(plan_row, got, panels, border)


def inverse_kernel(x_ref, table_ref, out_ref):
    owners = x_ref.shape[0]
    steps, receivers, width = out_ref.shape
    total = jnp.zeros((steps * receivers, width), F32)
    for owner in range(owners):
        total += jnp.dot(x_ref[owner], table_ref[owner], preferred_element_type=F32)
    out_ref[...] = total.astype(BF16).reshape(steps, receivers, width)


def inverse_of(spectra, table):
    owners, steps, receivers, cols = spectra.shape
    samples = table.shape[2]
    width = min(samples, 512)
    return pl.pallas_call(
        inverse_kernel,
        grid=(samples // width,),
        out_shape=jax.ShapeDtypeStruct((steps, receivers, samples), BF16),
        in_specs=[
            pl.BlockSpec((owners, steps * receivers, cols), lambda j: (0, 0, 0)),
            pl.BlockSpec((owners, cols, width), lambda j: (0, 0, j)),
        ],
        out_specs=pl.BlockSpec((steps, receivers, width), lambda j: (0, 0, j)),
        cost_estimate=pl.CostEstimate(
            flops=2 * owners * steps * receivers * cols * samples,
            bytes_accessed=2 * owners * cols * samples,
            transcendentals=0,
        ),
        compiler_params=pltpu.CompilerParams(vmem_limit_bytes=24 << 20),
        name="inverse_dft",
    )(spectra.reshape(owners, steps * receivers, cols), table)


def exchange(blocks):
    return lax.all_to_all(blocks, "line", split_axis=0, concat_axis=0, tiled=True)


def local(traces, owner, panel_index, receiver_slot, aperture_weight, panels, plan):
    owners = lax.axis_size("line")
    areas = lax.axis_size("area")
    rows, samples = traces.shape
    cols = 2 * NF // owners
    forward, inverse = make_tables(samples, NF, owners)
    forward = jnp.asarray(forward)
    inverse = jnp.asarray(inverse)
    plan_row = plan[lax.axis_index("area")]

    panel_blocks = exchange(transform_panel(panels[0, 0], forward))
    edges = jnp.stack([panel_blocks[plan_row[k], -EDGE:] for k in range(STEPS)], 0)
    border = lax.ppermute(edges, "area", [(i, i + 1) for i in range(areas - 1)])

    items = [owner[:, 0], receiver_slot, panel_index // BASE, panel_index % BASE]
    meta = jnp.stack(items, 0).reshape(-1, cols).astype(BF16)
    meta = jnp.pad(meta, ((0, META - meta.shape[0]), (0, 0)))
    got = exchange(transform_traces(traces, aperture_weight[:, None], meta, forward))

    sums = exchange(receivers_of(plan_row, got, panel_blocks, border))
    return inverse_of(sums, inverse)


def solution(mesh):
    in_specs = (
        P(("area", "line"), None),
        P(("area", "line"), None),
        P(("area", "line")),
        P(("area", "line")),
        P(("area", "line")),
        P("area", "line", None, None),
        P(),
    )
    out_specs = P(None, ("area", "line"), None)
    return jax.shard_map(local, mesh=mesh, in_specs=in_specs, out_specs=out_specs, check_vma=False)
```

```python
import functools
import math

import jax
import jax.numpy as jnp
import ml_dtypes
import numpy as np
from jax import lax
from jax.experimental import pallas as pl
from jax.experimental.pallas import tpu as pltpu
from jax.sharding import PartitionSpec as P

NF = 1024
EDGE = 64
STEPS = 4
RECV_DEV = 64
CHUNK = 2
INDEX_SPAN = 512
F32 = jnp.float32
BF16 = jnp.bfloat16
I32 = jnp.int32


def vmem():
    return pl.BlockSpec(memory_space=pltpu.VMEM)


def smem():
    return pl.BlockSpec(memory_space=pltpu.SMEM)


def params(mib):
    return pltpu.CompilerParams(vmem_limit_bytes=mib << 20)


@functools.lru_cache(maxsize=None)
def make_tables(samples, bins, owners):
    half = samples // 2
    each = bins // owners
    of_bins = np.arange(bins).reshape(bins // 2, 2).T.reshape(owners, each)
    ids = np.arange(half)[None, :, None] * of_bins[:, None, :] % samples
    phases = ids * (2.0 * math.pi / samples)
    scaling = 1.0 / math.sqrt(samples)
    both = np.concatenate([np.cos(phases), -np.sin(phases)], 2) * scaling
    doubled = np.where(of_bins == 0, 1.0, 2.0)
    forward = both.astype(ml_dtypes.bfloat16)
    inverse = both * np.concatenate([doubled, doubled], 1)[:, None, :]
    inverse = np.ascontiguousarray(inverse.transpose(0, 2, 1)).astype(ml_dtypes.bfloat16)
    return forward, inverse


def forward_kernel(chips, count, ids_ref, *refs):
    inputs, tables, outs = refs[:count], refs[count : count + chips], refs[count + chips :]
    sign = ids_ref[chips].astype(F32)
    for number, x_ref in enumerate(inputs):
        rows, samples = x_ref.shape
        low = x_ref[:, : samples // 2].astype(F32)
        high = x_ref[:, samples // 2 :].astype(F32) * sign
        folded = ((low + high).astype(BF16), (low - high).astype(BF16))
        for distance in range(chips):
            spectra = jnp.dot(
                folded[2 * distance // chips],
                tables[distance][0],
                preferred_element_type=F32,
            )
            outs[distance][number * rows : (number + 1) * rows, :] = spectra.astype(BF16)


def forward_of(ids, arrays, table, name):
    rows, samples = arrays[0].shape
    owners, half, cols = table.shape
    chips = owners // 2
    count = len(arrays)

    def table_spec(distance):
        return pl.BlockSpec((1, half, cols), lambda i, ids_ref: (ids_ref[distance], 0, 0))

    whole = pl.BlockSpec((rows, samples), lambda i, ids_ref: (0, 0))
    out = pl.BlockSpec((count * rows, cols), lambda i, ids_ref: (0, 0))
    return pl.pallas_call(
        functools.partial(forward_kernel, chips, count),
        grid_spec=pltpu.PrefetchScalarGridSpec(
            num_scalar_prefetch=1,
            grid=(1,),
            in_specs=[whole] * count + [table_spec(d) for d in range(chips)],
            out_specs=[out] * chips,
        ),
        out_shape=[jax.ShapeDtypeStruct((count * rows, cols), BF16)] * chips,
        cost_estimate=pl.CostEstimate(
            flops=2 * count * rows * half * cols * chips,
            bytes_accessed=2 * (half * cols * chips + count * rows * samples * 2),
            transcendentals=0,
        ),
        compiler_params=params(48),
        name=name,
    )(ids, *arrays, *[table] * chips)


def masks_kernel(ids_ref, facts_ref, gather_ref, summer_ref, weight_ref, rows_ref):
    owners, _, rows = facts_ref.shape
    chips = owners // 2
    chip, core = ids_ref[chips + 1], ids_ref[chips + 2]
    receivers = summer_ref.shape[0]
    extent = gather_ref.shape[1]
    for block in range(owners):
        line = (chip ^ (block // 2)) * 2 + (core ^ (block % 2))
        facts = facts_ref[line]
        packed = facts[0:1].astype(I32)
        index = packed % INDEX_SPAN
        slot = packed // INDEX_SPAN % RECV_DEV
        owner = packed // (INDEX_SPAN * RECV_DEV)
        place = (((owner // 2) ^ chip) * 2 + ((owner % 2) ^ core)) * RECV_DEV + slot
        ids = lax.broadcasted_iota(I32, (receivers, rows), 0)
        summer_ref[:, block * rows : (block + 1) * rows] = (ids == place).astype(BF16)
        rows_ref[block : block + 1, :] = index.astype(F32)
        rows_ref[owners + block : owners + block + 1, :] = facts[1:2]
    square = (rows, rows)
    eye = (
        lax.broadcasted_iota(I32, square, 0) == lax.broadcasted_iota(I32, square, 1)
    ).astype(F32)
    turned = lax.dot_general(
        eye,
        rows_ref[...],
        (((1,), (1,)), ((), ())),
        precision=lax.Precision.HIGHEST,
        preferred_element_type=F32,
    )
    weight_ref[...] = turned[:, owners:]
    ids = lax.broadcasted_iota(I32, (rows, extent), 1)
    for block in range(owners):
        index = turned[:, block : block + 1].astype(I32)
        gather_ref[block * rows : (block + 1) * rows, :] = (ids == index).astype(BF16)


def masks_of(ids, facts, extent):
    owners, _, rows = facts.shape
    return pl.pallas_call(
        masks_kernel,
        out_shape=[
            jax.ShapeDtypeStruct((owners * rows, extent), BF16),
            jax.ShapeDtypeStruct((owners * RECV_DEV, owners * rows), BF16),
            jax.ShapeDtypeStruct((rows, owners), F32),
        ],
        in_specs=[smem(), vmem()],
        out_specs=[vmem()] * 3,
        scratch_shapes=[pltpu.VMEM((2 * owners, rows), F32)],
        cost_estimate=pl.CostEstimate(
            flops=6 * owners * rows * (extent + owners * RECV_DEV),
            bytes_accessed=2 * owners * rows * (extent + owners * RECV_DEV),
            transcendentals=0,
        ),
        compiler_params=params(48),
        name="masks",
    )(ids, facts)


def choose_kernel(chosen_ref, *refs):
    blocks, main_ref, edges_ref = refs[:-2], refs[-2], refs[-1]
    for step in range(STEPS):
        for number, block in enumerate(blocks):

            @pl.when(chosen_ref[step] == number)
            def _():
                main_ref[step] = block[...]
                edges_ref[step] = block[block.shape[0] - EDGE :, :]


def choose(chosen, blocks):
    rows, cols = blocks[0].shape
    return pl.pallas_call(
        choose_kernel,
        out_shape=[
            jax.ShapeDtypeStruct((STEPS, rows, cols), BF16),
            jax.ShapeDtypeStruct((STEPS, EDGE, cols), BF16),
        ],
        in_specs=[smem()] + [vmem()] * len(blocks),
        out_specs=[vmem()] * 2,
        cost_estimate=pl.CostEstimate(
            flops=STEPS * rows * cols,
            bytes_accessed=2 * (len(blocks) + STEPS) * rows * cols,
            transcendentals=0,
        ),
        compiler_params=params(48),
        name="choose_panels",
    )(chosen, *blocks)


def product_kernel(first, chips, *refs):
    main_ref, border_ref, gather_ref, summer_ref, weight_ref = refs[:5]
    spectra_refs, outs = refs[5 : 5 + chips], refs[5 + chips :]
    cols = main_ref.shape[2]
    half = cols // 2
    rows = weight_ref.shape[0]
    receivers = summer_ref.shape[0]
    extended = [
        jnp.concatenate([main_ref[first + step], border_ref[first + step]], 0)
        for step in range(CHUNK)
    ]
    totals = [jnp.zeros((receivers, cols), F32) for _ in range(CHUNK)]
    for block in range(2 * chips):
        at = block * rows
        mine = block % 2 * rows
        spectra = spectra_refs[block // 2][mine : mine + rows, :].astype(F32)
        spectra = spectra * weight_ref[:, block : block + 1]
        real_d, imag_d = spectra[:, :half], spectra[:, half:]
        for step in range(CHUNK):
            picked = jnp.dot(
                gather_ref[at : at + rows, :], extended[step], preferred_element_type=F32
            )
            real_p, imag_p = picked[:, :half], picked[:, half:]
            product = jnp.concatenate(
                [real_p * real_d - imag_p * imag_d, real_p * imag_d + imag_p * real_d], 1
            ).astype(BF16)
            totals[step] += jnp.dot(
                summer_ref[:, at : at + rows], product, preferred_element_type=F32
            )
    for step in range(CHUNK):
        result = totals[step].astype(BF16)
        for place in range(2 * chips):
            rows_of = result[place * RECV_DEV : (place + 1) * RECV_DEV]
            outs[place // 2][place % 2, step] = rows_of


def receivers_of(first, main, border, gather, summer, weight, spectra):
    chips = len(spectra)
    cols = main.shape[2]
    return pl.pallas_call(
        functools.partial(product_kernel, first, chips),
        out_shape=[jax.ShapeDtypeStruct((2, CHUNK, RECV_DEV, cols), BF16)] * chips,
        in_specs=[vmem()] * (5 + chips),
        out_specs=[vmem()] * chips,
        cost_estimate=pl.CostEstimate(
            flops=2 * CHUNK * cols * gather.shape[0] * (gather.shape[1] + summer.shape[0]),
            bytes_accessed=2 * (gather.size + summer.size + gather.shape[0] * cols),
            transcendentals=0,
        ),
        compiler_params=params(48),
        name="receiver_sums",
    )(main, border, gather, summer, weight, *spectra)


def inverse_kernel(chips, ids_ref, *refs):
    per_chunk = chips + 1
    chunks = STEPS // CHUNK
    groups = [refs[i * per_chunk : (i + 1) * per_chunk] for i in range(chunks)]
    tables = refs[chunks * per_chunk : -1]
    out_ref = refs[-1]
    samples = out_ref.shape[2]
    width = tables[0].shape[2]
    cols = tables[0].shape[1]
    sign = ids_ref[2 * chips].astype(F32)
    sums = [None, None]
    for distance in range(chips):
        for across in range(2):
            parts = []
            for group in groups:
                part = group[distance][0] if across == 0 else group[chips][distance]
                parts.append(part.reshape(CHUNK * RECV_DEV, cols))
            term = jnp.dot(
                jnp.concatenate(parts, 0),
                tables[2 * distance + across][0],
                preferred_element_type=F32,
            )
            which = 2 * distance // chips
            sums[which] = term if sums[which] is None else sums[which] + term
    shape = (STEPS, RECV_DEV, width)
    at = pl.multiple_of(pl.program_id(0) * width, width)
    out_ref[:, :, pl.ds(at, width)] = (sums[0] + sums[1]).astype(BF16).reshape(shape)
    at = pl.multiple_of(pl.program_id(0) * width + samples // 2, width)
    out_ref[:, :, pl.ds(at, width)] = ((sums[0] - sums[1]) * sign).astype(BF16).reshape(shape)


def inverse_of(ids, groups, table):
    owners, cols, half = table.shape
    chips = owners // 2
    width = min(half, 256)
    arrays = [array for group in groups for array in group]

    def table_spec(block):
        return pl.BlockSpec((1, cols, width), lambda i, ids_ref: (ids_ref[block], 0, i))

    def whole(array):
        rank = array.ndim
        return pl.BlockSpec(array.shape, lambda i, ids_ref: (0,) * rank)

    return pl.pallas_call(
        functools.partial(inverse_kernel, chips),
        grid_spec=pltpu.PrefetchScalarGridSpec(
            num_scalar_prefetch=1,
            grid=(half // width,),
            in_specs=[whole(a) for a in arrays] + [table_spec(b) for b in range(owners)],
            out_specs=pl.BlockSpec((STEPS, RECV_DEV, 2 * half), lambda i, ids_ref: (0, 0, 0)),
        ),
        out_shape=jax.ShapeDtypeStruct((STEPS, RECV_DEV, 2 * half), BF16),
        cost_estimate=pl.CostEstimate(
            flops=2 * STEPS * RECV_DEV * owners * cols * half,
            bytes_accessed=2 * owners * cols * half,
            transcendentals=0,
        ),
        compiler_params=params(48),
        name="inverse_dft",
    )(ids, *arrays, *[table] * owners)


def swap(array, distance):
    devices = range(lax.axis_size("line"))
    return lax.ppermute(array, "line", [(i, i ^ distance) for i in devices])


def send_blocks(blocks):
    chips = len(blocks)
    sent = {d: swap(blocks[d], 2 * d) for d in range(chips - 1, 0, -1)}
    return [blocks[0]] + [sent[d] for d in range(1, chips)]


def local(traces, owner, panel_index, receiver_slot, aperture_weight, panels, plan):
    owners = lax.axis_size("line")
    areas = lax.axis_size("area")
    chips = owners // 2
    samples = traces.shape[1]
    panel = panels[0, 0]
    forward, inverse = make_tables(samples, NF, owners)
    forward = jnp.asarray(forward)
    inverse = jnp.asarray(inverse)

    line = lax.axis_index("line")
    chip, core = line // 2, line % 2
    sign = jnp.where(2 * chip < chips, 1, -1)
    near = [(chip ^ d) * 2 + core for d in range(chips)]
    near_ids = jnp.stack(near + [sign, chip, core]).astype(I32)
    all_ids = [(chip ^ (b // 2)) * 2 + (core ^ (b % 2)) for b in range(owners)]
    all_ids = jnp.stack(all_ids + [sign]).astype(I32)
    plan_row = plan[lax.axis_index("area")]
    chosen = ((plan_row // 2) ^ chip) * 2 + ((plan_row % 2) ^ core)

    panel_across = swap(panel, 1)
    traces_across = swap(traces, 1)
    packed = (owner[:, 0] * RECV_DEV + receiver_slot) * INDEX_SPAN + panel_index
    facts = jnp.stack([packed.astype(F32), aperture_weight], 0)
    facts = lax.all_gather(facts, "line")

    near_panels = send_blocks(forward_of(near_ids, [panel], forward, "panel_dft"))
    far_panels = send_blocks(forward_of(near_ids, [panel_across], forward, "panel_dft"))
    spectra = send_blocks(forward_of(near_ids, [traces, traces_across], forward, "trace_dft"))

    blocks = [block for pair in zip(near_panels, far_panels) for block in pair]
    main, edges = choose(chosen, blocks)
    border = lax.ppermute(edges, "area", [(i, i + 1) for i in range(areas - 1)])
    gather, summer, weight = masks_of(near_ids, facts, panel.shape[0] + EDGE)

    groups = []
    for first in range(0, STEPS, CHUNK):
        sums = receivers_of(first, main, border, gather, summer, weight, spectra)
        sums = send_blocks(sums)
        across = swap(jnp.stack([block[1] for block in sums]), 1)
        groups.append(sums + [across])
    return inverse_of(all_ids, groups, inverse)


def solution(mesh):
    in_specs = (
        P(("area", "line"), None),
        P(("area", "line"), None),
        P(("area", "line")),
        P(("area", "line")),
        P(("area", "line")),
        P("area", "line", None, None),
        P(),
    )
    out_specs = P(None, ("area", "line"), None)
    return jax.shard_map(local, mesh=mesh, in_specs=in_specs, out_specs=out_specs, check_vma=False)
```

```python
import functools
import math

import jax
import jax.numpy as jnp
import ml_dtypes
import numpy as np
from jax import lax
from jax.experimental import pallas as pl
from jax.experimental.pallas import tpu as pltpu
from jax.sharding import PartitionSpec as P

NF = 1024
EDGE = 64
STEPS = 4
RECV_DEV = 64
CHUNK = 2
BASE = 64
FACTS = 8
ROWS = 16
LANES = 128
F32 = jnp.float32
BF16 = jnp.bfloat16
I32 = jnp.int32


def vmem():
    return pl.BlockSpec(memory_space=pltpu.VMEM)


def hbm():
    return pl.BlockSpec(memory_space=pltpu.HBM)


def in_hbm(array):
    return pltpu.with_memory_space_constraint(array, pltpu.HBM)


def smem():
    return pl.BlockSpec(memory_space=pltpu.SMEM)


def params(mib):
    return pltpu.CompilerParams(vmem_limit_bytes=mib << 20)


@functools.lru_cache(maxsize=None)
def make_tables(samples, bins, owners):
    scaling = 1.0 / math.sqrt(samples)
    half, period, each = samples // 2, samples // owners, bins // owners
    of_bins = np.arange(bins).reshape(each, owners).T
    ids = np.arange(half)[None, :, None] * of_bins[:, None, :] % samples
    phases = ids * (2.0 * math.pi / samples)
    forward = np.concatenate([np.cos(phases), -np.sin(phases)], 2) * scaling
    phases = np.outer(np.arange(each), np.arange(period)) % period * (2.0 * math.pi / period)
    real, imag = np.cos(phases) * scaling, np.sin(phases) * scaling
    inverse = np.concatenate(
        [np.concatenate([real, imag], 1), np.concatenate([-imag, real], 1)], 0
    )
    inverse = np.stack([inverse, 2.0 * inverse])
    inverse[0, 1:each] *= 2.0
    inverse[0, each + 1 :] *= 2.0
    phases = np.outer(np.arange(owners), np.arange(period)) * (2.0 * math.pi / samples)
    turns = np.stack([np.cos(phases), np.sin(phases)], 1).astype(np.float32)
    return forward.astype(ml_dtypes.bfloat16), inverse.astype(ml_dtypes.bfloat16), turns


def facts_message(facts, height, cols):
    index, slot, owner, weight = [ref[...].astype(F32)[None, :] for ref in facts]
    high = index.astype(I32) // BASE
    first = weight.astype(BF16).astype(F32)
    second = (weight - first).astype(BF16).astype(F32)
    lines = [high.astype(F32), index - (high * BASE).astype(F32), slot, owner]
    lines += [first, second, weight - first - second, jnp.zeros_like(weight)]
    block = jnp.concatenate(lines, 0)
    parts = [block[:, at : at + cols] for at in range(0, block.shape[1], cols)]
    parts += [jnp.zeros((height - FACTS * len(parts), cols), F32)] * (height > FACTS * len(parts))
    return jnp.concatenate(parts, 0).astype(BF16)


def fold(x_ref, sign):
    half = x_ref.shape[1] // 2
    return (x_ref[:, :half].astype(F32) + x_ref[:, half:].astype(F32) * sign).astype(BF16)


def first_kernel(chips, ids_ref, table_ref, x_ref, *refs):
    given, (out_ref, folded_ref, held, message_ref) = refs[:4], refs[4:8]
    ready, taken, sems = refs[8], refs[9:13], refs[13]
    rows = x_ref.shape[0]
    far = chips - 1
    copies = [
        pltpu.make_async_copy(x_ref, ready, sems.at[0]),
        pltpu.make_async_copy(table_ref.at[ids_ref[far]], held.at[0], sems.at[1]),
    ]
    copies += [
        pltpu.make_async_copy(source, target, sems.at[2 + i])
        for i, (source, target) in enumerate(zip(given, taken))
    ]
    for copy in copies:
        copy.start()
    copies[0].wait()
    folded = fold(ready, ids_ref[chips].astype(F32))
    folded_ref[...] = folded
    for copy in copies[1:]:
        copy.wait()
    spectra = jnp.dot(folded, held[0], preferred_element_type=F32)
    out_ref[:rows, :] = spectra.astype(BF16)
    message = facts_message(taken, *message_ref.shape)
    message_ref[...] = message
    out_ref[rows:, :] = message


def second_kernel(chips, ids_ref, table_ref, folded_ref, message_ref, *refs):
    outs, held, sems = refs[: chips - 1], refs[chips - 1], refs[chips]
    rows = folded_ref.shape[0]
    copies = [
        pltpu.make_async_copy(table_ref.at[ids_ref[d]], held.at[d], sems.at[d])
        for d in range(chips - 1)
    ]
    for copy in copies[::-1]:
        copy.start()
    for out_ref in outs:
        out_ref[rows:, :] = message_ref[...]
    for d in range(chips - 2, -1, -1):
        copies[d].wait()
        spectra = jnp.dot(folded_ref[...], held[d], preferred_element_type=F32)
        outs[d][:rows, :] = spectra.astype(BF16)


def near_of(ids, panel, table, facts):
    rows, samples = panel.shape
    owners, half, cols = table.shape
    chips = owners // 2
    height = 2 * FACTS * -(-rows // (2 * cols))
    block = jax.ShapeDtypeStruct((rows + height, cols), BF16)
    table = in_hbm(table)

    def cost(count):
        return pl.CostEstimate(
            flops=2 * rows * half * cols * count,
            bytes_accessed=2 * (half * cols * count + rows * samples),
            transcendentals=0,
        )

    last, folded, held_last, message = pl.pallas_call(
        functools.partial(first_kernel, chips),
        out_shape=[
            block,
            jax.ShapeDtypeStruct((rows, half), BF16),
            jax.ShapeDtypeStruct((1, half, cols), BF16),
            jax.ShapeDtypeStruct((height, cols), BF16),
        ],
        in_specs=[smem()] + [hbm()] * 6,
        out_specs=[vmem()] * 4,
        scratch_shapes=[pltpu.VMEM((rows, samples), BF16)]
        + [pltpu.VMEM(fact.shape, fact.dtype) for fact in facts]
        + [pltpu.SemaphoreType.DMA((6,))],
        cost_estimate=cost(1),
        compiler_params=params(24),
        name="first_panel_dft",
    )(ids, table, in_hbm(panel), *[in_hbm(fact) for fact in facts])
    *blocks, held = pl.pallas_call(
        functools.partial(second_kernel, chips),
        out_shape=[block] * (chips - 1) + [jax.ShapeDtypeStruct((chips - 1, half, cols), BF16)],
        in_specs=[smem(), hbm(), vmem(), vmem()],
        out_specs=[vmem()] * chips,
        scratch_shapes=[pltpu.SemaphoreType.DMA((chips - 1,))],
        cost_estimate=cost(chips - 1),
        compiler_params=params(24),
        name="near_panel_dft",
    )(ids, table, folded, message)
    return blocks + [last], [held, held_last]


def forward_kernel(chips, count, ids_ref, table_ref, last_ref, *refs):
    inputs, outs = refs[:count], refs[count:]
    for number, x_ref in enumerate(inputs):
        rows = x_ref.shape[0]
        folded = fold(x_ref, ids_ref[chips].astype(F32))
        for d in range(chips - 1, -1, -1):
            table = last_ref[0] if d == chips - 1 else table_ref[d]
            spectra = jnp.dot(folded, table, preferred_element_type=F32)
            outs[d][number * rows : (number + 1) * rows, :] = spectra.astype(BF16)


def forward_of(ids, arrays, tables, name):
    rows, samples = arrays[0].shape
    half, cols = tables[0].shape[1:]
    chips = tables[0].shape[0] + 1
    count = len(arrays)
    return pl.pallas_call(
        functools.partial(forward_kernel, chips, count),
        out_shape=[jax.ShapeDtypeStruct((count * rows, cols), BF16)] * chips,
        in_specs=[smem()] + [vmem()] * (count + 2),
        out_specs=[vmem()] * chips,
        cost_estimate=pl.CostEstimate(
            flops=2 * count * rows * half * cols * chips,
            bytes_accessed=2 * count * rows * samples * 2,
            transcendentals=0,
        ),
        compiler_params=params(24),
        name=name,
    )(ids, *tables, *arrays)


def masks_kernel(rows, ids_ref, *refs):
    facts, (gather_ref, summer_ref, weight_ref) = refs[:2], refs[2:]
    chips, height, cols = facts[0].shape
    chip, core = ids_ref[chips + 1], ids_ref[chips + 2]
    receivers = summer_ref.shape[0]
    extent = gather_ref.shape[1]
    square = (cols, cols)
    eye = (
        lax.broadcasted_iota(I32, square, 0) == lax.broadcasted_iota(I32, square, 1)
    ).astype(BF16)
    places = lax.broadcasted_iota(I32, (receivers, cols), 0)
    indices = lax.broadcasted_iota(I32, (cols, extent), 1)
    stacked = jnp.concatenate(
        [facts[across][distance] for distance in range(chips) for across in range(2)], 0
    )
    every = lax.dot_general(eye, stacked, (((1,), (1,)), ((), ())), preferred_element_type=F32)
    for distance in range(chips):
        for across in range(2):
            wide = facts[across][distance].astype(F32).astype(I32)
            where = 2 * distance + across
            turned = every[:, where * height : (where + 1) * height]
            for part in range(rows // cols):
                line = part * FACTS
                at = where * rows + part * cols
                slot, owner = wide[line + 2 : line + 3], wide[line + 3 : line + 4]
                place = (((owner >> 1) ^ chip) * 2 + ((owner & 1) ^ core)) * RECV_DEV + slot
                summer_ref[:, at : at + cols] = (places == place).astype(BF16)
                column = [turned[:, line + i : line + i + 1] for i in range(7)]
                index = (column[0] * BASE + column[1]).astype(I32)
                gather_ref[at : at + cols, :] = (indices == index).astype(BF16)
                weight = column[4] + column[5] + column[6]
                weight_ref[part * cols : (part + 1) * cols, where : where + 1] = weight


def masks_of(ids, facts, rows, extent):
    chips = facts[0].shape[0]
    traces = 2 * chips * rows
    receivers = 2 * chips * RECV_DEV
    return pl.pallas_call(
        functools.partial(masks_kernel, rows),
        out_shape=[
            jax.ShapeDtypeStruct((traces, extent), BF16),
            jax.ShapeDtypeStruct((receivers, traces), BF16),
            jax.ShapeDtypeStruct((rows, 2 * chips), F32),
        ],
        in_specs=[smem()] + [vmem()] * 2,
        out_specs=[vmem()] * 3,
        cost_estimate=pl.CostEstimate(
            flops=6 * traces * (extent + receivers),
            bytes_accessed=2 * traces * (extent + receivers),
            transcendentals=0,
        ),
        compiler_params=params(24),
        name="masks",
    )(ids, *facts)


def choose_kernel(rows, ids_ref, plan_ref, *refs):
    blocks, (main_ref, edges_ref, facts_ref) = refs[:-3], refs[-3:]
    chips = len(blocks) // 2
    for number in range(chips):
        facts_ref[number] = blocks[2 * number][rows:, :]
    for step in range(STEPS):
        planned = plan_ref[ids_ref[chips + 3], step]
        chosen = ((planned >> 1) ^ ids_ref[chips + 1]) * 2 + ((planned & 1) ^ ids_ref[chips + 2])
        for number, block in enumerate(blocks):

            @pl.when(chosen == number)
            def _():
                main_ref[step] = block[:rows, :]
                edges_ref[step] = block[rows - EDGE : rows, :]


def choose(ids, plan, blocks):
    rows, cols = blocks[1].shape
    height = blocks[0].shape[0] - rows
    return pl.pallas_call(
        functools.partial(choose_kernel, rows),
        out_shape=[
            jax.ShapeDtypeStruct((STEPS, rows, cols), BF16),
            jax.ShapeDtypeStruct((STEPS, EDGE, cols), BF16),
            jax.ShapeDtypeStruct((len(blocks) // 2, height, cols), BF16),
        ],
        in_specs=[smem(), smem()] + [vmem()] * len(blocks),
        out_specs=[vmem()] * 3,
        cost_estimate=pl.CostEstimate(
            flops=STEPS * rows * cols,
            bytes_accessed=2 * STEPS * rows * cols,
            transcendentals=0,
        ),
        compiler_params=params(24),
        name="choose_panels",
    )(ids, plan, *blocks)


def product_kernel(first, chips, *refs):
    main_ref, border_ref, gather_ref, summer_ref, weight_ref = refs[:5]
    spectra_refs, outs = refs[5 : 5 + chips], refs[5 + chips :]
    cols = main_ref.shape[2]
    half = cols // 2
    rows = weight_ref.shape[0]
    receivers = summer_ref.shape[0]
    extended = [
        jnp.concatenate([main_ref[first + step], border_ref[first + step]], 0)
        for step in range(CHUNK)
    ]
    totals = [jnp.zeros((receivers, cols), F32) for _ in range(CHUNK)]
    for block in range(2 * chips):
        at = block * rows
        mine = block % 2 * rows
        spectra = spectra_refs[block // 2][mine : mine + rows, :].astype(F32)
        spectra = spectra * weight_ref[:, block : block + 1]
        real_d, imag_d = spectra[:, :half], spectra[:, half:]
        for step in range(CHUNK):
            picked = jnp.dot(
                gather_ref[at : at + rows, :], extended[step], preferred_element_type=F32
            )
            real_p, imag_p = picked[:, :half], picked[:, half:]
            product = jnp.concatenate(
                [real_p * real_d - imag_p * imag_d, real_p * imag_d + imag_p * real_d], 1
            ).astype(BF16)
            totals[step] += jnp.dot(
                summer_ref[:, at : at + rows], product, preferred_element_type=F32
            )
    for step in range(CHUNK):
        result = totals[step].astype(BF16)
        for place in range(2 * chips):
            rows_of = result[place * RECV_DEV : (place + 1) * RECV_DEV]
            outs[place // 2][place % 2, step] = rows_of


def receivers_of(first, main, border, gather, summer, weight, spectra):
    chips = len(spectra)
    cols = main.shape[2]
    return pl.pallas_call(
        functools.partial(product_kernel, first, chips),
        out_shape=[jax.ShapeDtypeStruct((2, CHUNK, RECV_DEV, cols), BF16)] * chips,
        in_specs=[vmem()] * (5 + chips),
        out_specs=[vmem()] * chips,
        cost_estimate=pl.CostEstimate(
            flops=2 * CHUNK * cols * gather.shape[0] * (gather.shape[1] + summer.shape[0]),
            bytes_accessed=2 * (gather.size + summer.size + gather.shape[0] * cols),
            transcendentals=0,
        ),
        compiler_params=params(24),
        name="receiver_sums",
    )(main, border, gather, summer, weight, *spectra)


def weighted_sum(terms):
    by_size = {}
    for coefficient, term in terms:
        size = round(abs(coefficient), 12)
        if size == 0.0:
            continue
        before = by_size.get(size)
        if before is None:
            by_size[size] = (term, coefficient)
        elif (before[1] < 0) == (coefficient < 0):
            by_size[size] = (before[0] + term, before[1])
        else:
            by_size[size] = (before[0] - term, before[1])
    total = None
    for term, coefficient in by_size.values():
        if abs(abs(coefficient) - 1.0) > 1e-9:
            term = term * coefficient
        elif coefficient < 0:
            term = -term
        total = term if total is None else total + term
    return total


def inverse_kernel(chips, ids_ref, table_ref, turns_ref, *refs):
    out_ref, real_ref, imag_ref = refs[-3:]
    owners, _, period = turns_ref.shape
    cols = table_ref.shape[1]
    per_chunk = chips + 1
    groups = [refs[i * per_chunk : (i + 1) * per_chunk] for i in range(STEPS // CHUNK)]
    for distance in range(chips):
        for across in range(2):
            parts = []
            for group in groups:
                part = group[distance][0] if across == 0 else group[chips][distance]
                parts.append(part.reshape(CHUNK * RECV_DEV, cols))
            line = ids_ref[2 * distance + across]
            spread = jnp.dot(
                jnp.concatenate(parts, 0),
                table_ref[jnp.minimum(line, 1)],
                preferred_element_type=F32,
            )
            real, imag = spread[:, :period], spread[:, period:]
            turn = turns_ref[line]
            real_ref[line] = real * turn[0:1] - imag * turn[1:2]
            imag_ref[line] = real * turn[1:2] + imag * turn[0:1]

    angles = [[2.0 * math.pi * (r * q % owners) / owners for r in range(owners)] for q in range(owners)]

    @pl.loop(0, STEPS * RECV_DEV // ROWS)
    def _(chunk):
        at = pl.multiple_of(chunk * ROWS, ROWS)
        step = at // RECV_DEV
        row = pl.multiple_of(at % RECV_DEV, ROWS)
        for lane in range(0, period, LANES):
            lanes = slice(lane, min(lane + LANES, period))
            real = [real_ref[r, pl.ds(at, ROWS), lanes] for r in range(owners)]
            imag = [imag_ref[r, pl.ds(at, ROWS), lanes] for r in range(owners)]
            for q in range(owners // 2):
                sums = []
                for parity in range(2):
                    terms = []
                    for r in range(parity, owners, 2):
                        terms += [(math.cos(angles[q][r]), real[r])]
                        terms += [(-math.sin(angles[q][r]), imag[r])]
                    sums.append(weighted_sum(terms))
                for value, place in ((sums[0] + sums[1], q), (sums[0] - sums[1], q + owners // 2)):
                    start = place * period + lane
                    out_ref[step, pl.ds(row, ROWS), start : start + lanes.stop - lane] = (
                        value.astype(BF16)
                    )


def inverse_of(ids, groups, table, turns):
    owners, _, period = turns.shape
    arrays = [array for group in groups for array in group]
    rows = STEPS * RECV_DEV
    return pl.pallas_call(
        functools.partial(inverse_kernel, owners // 2),
        in_specs=[smem()] + [vmem()] * (2 + len(arrays)),
        out_specs=vmem(),
        out_shape=jax.ShapeDtypeStruct((STEPS, RECV_DEV, owners * period), BF16),
        scratch_shapes=[pltpu.VMEM((owners, rows, period), F32)] * 2,
        cost_estimate=pl.CostEstimate(
            flops=2 * rows * owners * table[0].size,
            bytes_accessed=2 * rows * owners * period,
            transcendentals=0,
        ),
        compiler_params=params(24),
        name="inverse_dft",
    )(ids, table, turns, *arrays)


def swap(array, distance):
    devices = range(lax.axis_size("line"))
    return lax.ppermute(array, "line", [(i, i ^ distance) for i in devices])


def send_blocks(blocks):
    chips = len(blocks)
    sent = {d: swap(blocks[d], 2 * d) for d in range(chips - 1, 0, -1)}
    return [blocks[0]] + [sent[d] for d in range(1, chips)]


def local(traces, owner, panel_index, receiver_slot, aperture_weight, panels, plan):
    owners = lax.axis_size("line")
    areas = lax.axis_size("area")
    chips = owners // 2
    samples = traces.shape[1]
    panel = panels[0, 0]
    forward, inverse, turns = make_tables(samples, NF, owners)
    forward = jnp.asarray(forward)
    inverse = jnp.asarray(inverse)
    turns = jnp.asarray(turns)

    line = lax.axis_index("line")
    chip, core = lax.shift_right_logical(line, 1), line & 1
    sign = 1 - 2 * core
    near = [(chip ^ d) * 2 + core for d in range(chips)]
    near_ids = jnp.stack(near + [sign, chip, core, lax.axis_index("area")]).astype(I32)
    all_ids = [(chip ^ (b // 2)) * 2 + (core ^ (b % 2)) for b in range(owners)]
    all_ids = jnp.stack(all_ids).astype(I32)

    panel_across = swap(panel, 1)
    traces_across = swap(traces, 1)
    facts = [panel_index, receiver_slot, owner.reshape(-1), aperture_weight]
    near_panels, tables = near_of(near_ids, panel, forward, facts)
    near_panels = send_blocks(near_panels)
    far_panels = forward_of(near_ids, [panel_across], tables, "far_panel_dft")
    far_panels = send_blocks(far_panels)
    spectra = forward_of(near_ids, [traces, traces_across], tables, "trace_dft")
    spectra = send_blocks(spectra)

    blocks = [block for pair in zip(near_panels, far_panels) for block in pair]
    main, edges, near_facts = choose(near_ids, plan, blocks)
    facts = [near_facts, swap(near_facts, 1)]
    border = lax.ppermute(edges, "area", [(i, i + 1) for i in range(areas - 1)])
    gather, summer, weight = masks_of(near_ids, facts, panel.shape[0], panel.shape[0] + EDGE)

    groups = []
    for first in range(0, STEPS, CHUNK):
        sums = receivers_of(first, main, border, gather, summer, weight, spectra)
        sums = send_blocks(sums)
        across = swap(jnp.stack([block[1] for block in sums]), 1)
        groups.append(sums + [across])
    return inverse_of(all_ids, groups, inverse, turns)


def solution(mesh):
    in_specs = (
        P(("area", "line"), None),
        P(("area", "line"), None),
        P(("area", "line")),
        P(("area", "line")),
        P(("area", "line")),
        P("area", "line", None, None),
        P(),
    )
    out_specs = P(None, ("area", "line"), None)
    return jax.shard_map(local, mesh=mesh, in_specs=in_specs, out_specs=out_specs, check_vma=False)
```

```python
import functools
import math

import jax
import jax.numpy as jnp
import ml_dtypes
import numpy as np
from jax import lax
from jax.experimental import pallas as pl
from jax.experimental.pallas import tpu as pltpu
from jax.sharding import PartitionSpec as P

NF = 1024
EDGE = 64
STEPS = 4
RECV_DEV = 64
CHUNK = 2
BASE = 64
FACTS = 8
ROWS = 16
LANES = 128
F32 = jnp.float32
BF16 = jnp.bfloat16
I32 = jnp.int32


def vmem():
    return pl.BlockSpec(memory_space=pltpu.VMEM)


def hbm():
    return pl.BlockSpec(memory_space=pltpu.HBM)


def in_hbm(array):
    return pltpu.with_memory_space_constraint(array, pltpu.HBM)


def smem():
    return pl.BlockSpec(memory_space=pltpu.SMEM)


def params(mib):
    return pltpu.CompilerParams(vmem_limit_bytes=mib << 20)


@functools.lru_cache(maxsize=None)
def make_tables(samples, bins, owners):
    scaling = 1.0 / math.sqrt(samples)
    half, period, each = samples // 2, samples // owners, bins // owners
    ids = np.arange(half).reshape(1, half // period, period)
    ids = ids * np.arange(owners)[:, None, None] % samples
    forward_turns = ids * (2.0 * math.pi / samples)
    forward_turns = np.concatenate([np.cos(forward_turns), -np.sin(forward_turns)], 1)
    phases = np.outer(np.arange(each), np.arange(period)) % period * (2.0 * math.pi / period)
    real, imag = np.cos(phases) * scaling, np.sin(phases) * scaling
    inverse = np.concatenate(
        [np.concatenate([real, imag], 1), np.concatenate([-imag, real], 1)], 0
    )
    forward = inverse.T
    inverse = np.stack([inverse, 2.0 * inverse])
    inverse[0, 1:each] *= 2.0
    inverse[0, each + 1 :] *= 2.0
    phases = np.outer(np.arange(owners), np.arange(period)) * (2.0 * math.pi / samples)
    turns = np.stack([np.cos(phases), np.sin(phases)], 1).astype(np.float32)
    forward = np.ascontiguousarray(forward).astype(ml_dtypes.bfloat16)
    return forward, forward_turns.astype(np.float32), inverse.astype(ml_dtypes.bfloat16), turns


def facts_message(facts, height, cols):
    index, slot, owner, weight = [ref[...].astype(F32)[None, :] for ref in facts]
    high = index.astype(I32) // BASE
    first = weight.astype(BF16).astype(F32)
    second = (weight - first).astype(BF16).astype(F32)
    lines = [high.astype(F32), index - (high * BASE).astype(F32), slot, owner]
    lines += [first, second, weight - first - second, jnp.zeros_like(weight)]
    block = jnp.concatenate(lines, 0)
    parts = [block[:, at : at + cols] for at in range(0, block.shape[1], cols)]
    parts += [jnp.zeros((height - FACTS * len(parts), cols), F32)] * (height > FACTS * len(parts))
    return jnp.concatenate(parts, 0).astype(BF16)


def spread_turns(chips, ids_ref, turns_ref, wide_ref):
    for d in range(chips):
        turn = turns_ref[ids_ref[d]]
        for number in range(turn.shape[0]):
            wide_ref[d, number] = jnp.broadcast_to(turn[number : number + 1], wide_ref.shape[2:])


def turn_rows(ids_ref, x_ref, base, count, wide_ref, y_ref, at):
    chips, owners, _, period = wide_ref.shape
    half = owners // 2
    sign = ids_ref[chips].astype(F32)

    @pl.loop(0, count // ROWS)
    def _(chunk):
        row = pl.multiple_of(base + chunk * ROWS, ROWS)
        to = pl.multiple_of(at + chunk * ROWS, ROWS)
        for lane in range(0, period, LANES):
            stop = min(lane + LANES, period)
            folded = []
            for q in range(half):
                low = x_ref[pl.ds(row, ROWS), q * period + lane : q * period + stop]
                start = (q + half) * period
                high = x_ref[pl.ds(row, ROWS), start + lane : start + stop]
                folded.append(low.astype(F32) + high.astype(F32) * sign)
            for d in range(chips):
                for part in range(2):
                    total = folded[0] * wide_ref[d, part * half, :, lane:stop]
                    for q in range(1, half):
                        total += folded[q] * wide_ref[d, part * half + q, :, lane:stop]
                    start = part * period
                    y_ref[d, pl.ds(to, ROWS), start + lane : start + stop] = total.astype(BF16)


def first_kernel(chips, ids_ref, table_ref, turns_ref, x_ref, *refs):
    given, outs, (table, wide), refs = refs[:4], refs[4:][:chips], refs[4 + chips :][:2], refs[6 + chips :]
    turns, ready, taken, (y_ref, sems) = refs[0], refs[1], refs[2:6], refs[6:]
    rows = x_ref.shape[0]
    part = rows // 2
    pairs = [(turns_ref, turns)]
    pairs += [(x_ref.at[pl.ds(at, part)], ready.at[pl.ds(at, part)]) for at in (0, part)]
    pairs += [(table_ref, table), *zip(given, taken)]
    copies = [
        pltpu.make_async_copy(source, target, sems.at[i]) for i, (source, target) in enumerate(pairs)
    ]
    for copy in copies:
        copy.start()
    copies[0].wait()
    spread_turns(chips, ids_ref, turns, wide)
    for number in range(2):
        copies[1 + number].wait()
        turn_rows(ids_ref, ready, number * part, part, wide, y_ref, number * part)
    for copy in copies[3:]:
        copy.wait()
    message = facts_message(taken, outs[0].shape[0] - rows, outs[0].shape[1])
    for d in range(chips - 1, -1, -1):
        spectra = jnp.dot(y_ref[d], table[...], preferred_element_type=F32)
        outs[d][:rows, :] = spectra.astype(BF16)
        outs[d][rows:, :] = message


def cost_of(rows, table, turns):
    return pl.CostEstimate(
        flops=rows * turns.shape[0] * table.size,
        bytes_accessed=4 * rows * table.size // 64,
        transcendentals=0,
    )


def near_of(ids, panel, table, turns, facts):
    rows, samples = panel.shape
    cols = table.shape[1]
    chips = turns.shape[0] // 2
    owners, _, period = turns.shape
    height = 2 * FACTS * -(-rows // (2 * cols))
    return pl.pallas_call(
        functools.partial(first_kernel, chips),
        out_shape=[jax.ShapeDtypeStruct((rows + height, cols), BF16)] * chips
        + [
            jax.ShapeDtypeStruct(table.shape, BF16),
            jax.ShapeDtypeStruct((chips, owners, ROWS, period), F32),
        ],
        in_specs=[smem()] + [hbm()] * 7,
        out_specs=[vmem()] * (chips + 2),
        scratch_shapes=[pltpu.VMEM(turns.shape, F32), pltpu.VMEM((rows, samples), BF16)]
        + [pltpu.VMEM(fact.shape, fact.dtype) for fact in facts]
        + [pltpu.VMEM((chips, rows, 2 * period), BF16), pltpu.SemaphoreType.DMA((8,))],
        cost_estimate=cost_of(rows, table, turns),
        compiler_params=params(24),
        name="near_panel_dft",
    )(ids, *[in_hbm(array) for array in (table, turns, panel, *facts)])


def forward_kernel(chips, count, ids_ref, table_ref, wide, *refs):
    inputs, outs, y_ref = refs[:count], refs[count:-1], refs[-1]
    for number, x_ref in enumerate(inputs):
        rows = x_ref.shape[0]
        turn_rows(ids_ref, x_ref, 0, rows, wide, y_ref, number * rows)
    for d in range(chips - 1, -1, -1):
        outs[d][...] = jnp.dot(
            y_ref[d], table_ref[...], preferred_element_type=F32
        ).astype(BF16)


def forward_of(ids, arrays, table, wide, name):
    rows = len(arrays) * arrays[0].shape[0]
    cols = table.shape[1]
    chips, _, _, period = wide.shape
    count = len(arrays)
    return pl.pallas_call(
        functools.partial(forward_kernel, chips, count),
        out_shape=[jax.ShapeDtypeStruct((rows, cols), BF16)] * chips,
        in_specs=[smem()] + [vmem()] * (count + 2),
        out_specs=[vmem()] * chips,
        scratch_shapes=[pltpu.VMEM((chips, rows, 2 * period), BF16)],
        cost_estimate=cost_of(rows, table, wide),
        compiler_params=params(24),
        name=name,
    )(ids, table, wide, *arrays)


def masks_kernel(rows, ids_ref, *refs):
    facts, (gather_ref, summer_ref, weight_ref) = refs[:2], refs[2:]
    chips, height, cols = facts[0].shape
    chip, core = ids_ref[chips + 1], ids_ref[chips + 2]
    receivers = summer_ref.shape[0]
    extent = gather_ref.shape[1]
    square = (cols, cols)
    eye = (
        lax.broadcasted_iota(I32, square, 0) == lax.broadcasted_iota(I32, square, 1)
    ).astype(BF16)
    places = lax.broadcasted_iota(I32, (receivers, cols), 0)
    indices = lax.broadcasted_iota(I32, (cols, extent), 1)
    stacked = jnp.concatenate(
        [facts[across][distance] for distance in range(chips) for across in range(2)], 0
    )
    every = lax.dot_general(eye, stacked, (((1,), (1,)), ((), ())), preferred_element_type=F32)
    for distance in range(chips):
        for across in range(2):
            wide = facts[across][distance].astype(F32).astype(I32)
            where = 2 * distance + across
            turned = every[:, where * height : (where + 1) * height]
            for part in range(rows // cols):
                line = part * FACTS
                at = where * rows + part * cols
                slot, owner = wide[line + 2 : line + 3], wide[line + 3 : line + 4]
                place = (((owner >> 1) ^ chip) * 2 + ((owner & 1) ^ core)) * RECV_DEV + slot
                summer_ref[:, at : at + cols] = (places == place).astype(BF16)
                column = [turned[:, line + i : line + i + 1] for i in range(7)]
                index = (column[0] * BASE + column[1]).astype(I32)
                gather_ref[at : at + cols, :] = (indices == index).astype(BF16)
                weight = column[4] + column[5] + column[6]
                weight_ref[part * cols : (part + 1) * cols, where : where + 1] = weight


def masks_of(ids, facts, rows, extent):
    chips = facts[0].shape[0]
    traces = 2 * chips * rows
    receivers = 2 * chips * RECV_DEV
    return pl.pallas_call(
        functools.partial(masks_kernel, rows),
        out_shape=[
            jax.ShapeDtypeStruct((traces, extent), BF16),
            jax.ShapeDtypeStruct((receivers, traces), BF16),
            jax.ShapeDtypeStruct((rows, 2 * chips), F32),
        ],
        in_specs=[smem()] + [vmem()] * 2,
        out_specs=[vmem()] * 3,
        cost_estimate=pl.CostEstimate(
            flops=6 * traces * (extent + receivers),
            bytes_accessed=2 * traces * (extent + receivers),
            transcendentals=0,
        ),
        compiler_params=params(24),
        name="masks",
    )(ids, *facts)


def choose_kernel(rows, ids_ref, plan_ref, *refs):
    blocks, (main_ref, edges_ref, facts_ref) = refs[:-3], refs[-3:]
    chips = len(blocks) // 2
    for number in range(chips):
        facts_ref[number] = blocks[2 * number][rows:, :]
    for step in range(STEPS):
        planned = plan_ref[ids_ref[chips + 3], step]
        chosen = ((planned >> 1) ^ ids_ref[chips + 1]) * 2 + ((planned & 1) ^ ids_ref[chips + 2])
        for number, block in enumerate(blocks):

            @pl.when(chosen == number)
            def _():
                main_ref[step] = block[:rows, :]
                edges_ref[step] = block[rows - EDGE : rows, :]


def choose(ids, plan, blocks):
    rows, cols = blocks[1].shape
    height = blocks[0].shape[0] - rows
    return pl.pallas_call(
        functools.partial(choose_kernel, rows),
        out_shape=[
            jax.ShapeDtypeStruct((STEPS, rows, cols), BF16),
            jax.ShapeDtypeStruct((STEPS, EDGE, cols), BF16),
            jax.ShapeDtypeStruct((len(blocks) // 2, height, cols), BF16),
        ],
        in_specs=[smem(), smem()] + [vmem()] * len(blocks),
        out_specs=[vmem()] * 3,
        cost_estimate=pl.CostEstimate(
            flops=STEPS * rows * cols,
            bytes_accessed=2 * STEPS * rows * cols,
            transcendentals=0,
        ),
        compiler_params=params(24),
        name="choose_panels",
    )(ids, plan, *blocks)


def add_products(steps, distances, main_ref, border_ref, masks, spectra_refs, totals):
    gather_ref, summer_ref, weight_ref = masks
    half = main_ref.shape[2] // 2
    rows = weight_ref.shape[0]
    extended = [jnp.concatenate([main_ref[k], border_ref[k]], 0) for k in steps]
    for distance, spectra_ref in zip(distances, spectra_refs):
        for across in range(2):
            block = 2 * distance + across
            at = block * rows
            spectra = spectra_ref[across * rows : (across + 1) * rows, :].astype(F32)
            spectra = spectra * weight_ref[:, block : block + 1]
            real_d, imag_d = spectra[:, :half], spectra[:, half:]
            for number in range(len(steps)):
                picked = jnp.dot(
                    gather_ref[at : at + rows, :], extended[number], preferred_element_type=F32
                )
                real_p, imag_p = picked[:, :half], picked[:, half:]
                product = jnp.concatenate(
                    [real_p * real_d - imag_p * imag_d, real_p * imag_d + imag_p * real_d], 1
                ).astype(BF16)
                part = jnp.dot(
                    summer_ref[:, at : at + rows], product, preferred_element_type=F32
                )
                totals[number] = part if totals[number] is None else totals[number] + part
    return totals


def early_kernel(distances, main_ref, border_ref, *refs):
    masks, spectra_refs, partial_ref = refs[:3], refs[3:-1], refs[-1]
    for first in range(0, STEPS, CHUNK):
        steps = range(first, first + CHUNK)
        totals = [None] * CHUNK
        add_products(steps, distances, main_ref, border_ref, masks, spectra_refs, totals)
        for number, step in enumerate(steps):
            partial_ref[step] = totals[number]


def early_sums(distances, main, border, masks, spectra):
    cols = main.shape[2]
    gather, summer, _ = masks
    traces = len(spectra) * spectra[0].shape[0]
    return pl.pallas_call(
        functools.partial(early_kernel, distances),
        out_shape=jax.ShapeDtypeStruct((STEPS, summer.shape[0], cols), F32),
        in_specs=[vmem()] * (5 + len(spectra)),
        out_specs=vmem(),
        cost_estimate=pl.CostEstimate(
            flops=2 * STEPS * cols * traces * (gather.shape[1] + summer.shape[0]),
            bytes_accessed=2 * traces * cols,
            transcendentals=0,
        ),
        compiler_params=params(24),
        name="early_sums",
    )(main, border, *masks, *spectra)


def late_kernel(first, chips, distances, main_ref, border_ref, partial_ref, *refs):
    masks, spectra_refs, outs = refs[:3], refs[3:-chips], refs[-chips:]
    steps = range(first, first + CHUNK)
    totals = [partial_ref[step] for step in steps]
    add_products(steps, distances, main_ref, border_ref, masks, spectra_refs, totals)
    for number in range(CHUNK):
        result = totals[number].astype(BF16)
        for place in range(2 * chips):
            rows_of = result[place * RECV_DEV : (place + 1) * RECV_DEV]
            outs[place // 2][place % 2, number] = rows_of


def late_sums(first, chips, distances, main, border, partial, masks, spectra):
    cols = main.shape[2]
    gather, summer, _ = masks
    traces = len(spectra) * spectra[0].shape[0]
    return pl.pallas_call(
        functools.partial(late_kernel, first, chips, distances),
        out_shape=[jax.ShapeDtypeStruct((2, CHUNK, RECV_DEV, cols), BF16)] * chips,
        in_specs=[vmem()] * (6 + len(spectra)),
        out_specs=[vmem()] * chips,
        cost_estimate=pl.CostEstimate(
            flops=2 * CHUNK * cols * traces * (gather.shape[1] + summer.shape[0]),
            bytes_accessed=2 * traces * cols,
            transcendentals=0,
        ),
        compiler_params=params(24),
        name="receiver_sums",
    )(main, border, partial, *masks, *spectra)


def weighted_sum(terms):
    by_size = {}
    for coefficient, term in terms:
        size = round(abs(coefficient), 12)
        if size == 0.0:
            continue
        before = by_size.get(size)
        if before is None:
            by_size[size] = (term, coefficient)
        elif (before[1] < 0) == (coefficient < 0):
            by_size[size] = (before[0] + term, before[1])
        else:
            by_size[size] = (before[0] - term, before[1])
    total = None
    for term, coefficient in by_size.values():
        if abs(abs(coefficient) - 1.0) > 1e-9:
            term = term * coefficient
        elif coefficient < 0:
            term = -term
        total = term if total is None else total + term
    return total


def inverse_kernel(chips, ids_ref, table_ref, turns_ref, *refs):
    out_ref, real_ref, imag_ref = refs[-3:]
    owners, _, period = turns_ref.shape
    cols = table_ref.shape[1]
    per_chunk = chips + 1
    groups = [refs[i * per_chunk : (i + 1) * per_chunk] for i in range(STEPS // CHUNK)]
    for distance in range(chips):
        for across in range(2):
            parts = []
            for group in groups:
                part = group[distance][0] if across == 0 else group[chips][distance]
                parts.append(part.reshape(CHUNK * RECV_DEV, cols))
            line = ids_ref[2 * distance + across]
            spread = jnp.dot(
                jnp.concatenate(parts, 0),
                table_ref[jnp.minimum(line, 1)],
                preferred_element_type=F32,
            )
            real, imag = spread[:, :period], spread[:, period:]
            turn = turns_ref[line]
            real_ref[line] = real * turn[0:1] - imag * turn[1:2]
            imag_ref[line] = real * turn[1:2] + imag * turn[0:1]

    angles = [[2.0 * math.pi * (r * q % owners) / owners for r in range(owners)] for q in range(owners)]

    @pl.loop(0, STEPS * RECV_DEV // ROWS)
    def _(chunk):
        at = pl.multiple_of(chunk * ROWS, ROWS)
        step = at // RECV_DEV
        row = pl.multiple_of(at % RECV_DEV, ROWS)
        for lane in range(0, period, LANES):
            lanes = slice(lane, min(lane + LANES, period))
            real = [real_ref[r, pl.ds(at, ROWS), lanes] for r in range(owners)]
            imag = [imag_ref[r, pl.ds(at, ROWS), lanes] for r in range(owners)]
            for q in range(owners // 2):
                sums = []
                for parity in range(2):
                    terms = []
                    for r in range(parity, owners, 2):
                        terms += [(math.cos(angles[q][r]), real[r])]
                        terms += [(-math.sin(angles[q][r]), imag[r])]
                    sums.append(weighted_sum(terms))
                for value, place in ((sums[0] + sums[1], q), (sums[0] - sums[1], q + owners // 2)):
                    start = place * period + lane
                    out_ref[step, pl.ds(row, ROWS), start : start + lanes.stop - lane] = (
                        value.astype(BF16)
                    )


def inverse_of(ids, groups, table, turns):
    owners, _, period = turns.shape
    arrays = [array for group in groups for array in group]
    rows = STEPS * RECV_DEV
    return pl.pallas_call(
        functools.partial(inverse_kernel, owners // 2),
        in_specs=[smem()] + [vmem()] * (2 + len(arrays)),
        out_specs=vmem(),
        out_shape=jax.ShapeDtypeStruct((STEPS, RECV_DEV, owners * period), BF16),
        scratch_shapes=[pltpu.VMEM((owners, rows, period), F32)] * 2,
        cost_estimate=pl.CostEstimate(
            flops=2 * rows * owners * table[0].size,
            bytes_accessed=2 * rows * owners * period,
            transcendentals=0,
        ),
        compiler_params=params(24),
        name="inverse_dft",
    )(ids, table, turns, *arrays)


def swap(array, distance):
    devices = range(lax.axis_size("line"))
    return lax.ppermute(array, "line", [(i, i ^ distance) for i in devices])


def send_blocks(blocks):
    chips = len(blocks)
    sent = {d: swap(blocks[d], 2 * d) for d in range(chips - 1, 0, -1)}
    return [blocks[0]] + [sent[d] for d in range(1, chips)]


def local(traces, owner, panel_index, receiver_slot, aperture_weight, panels, plan):
    owners = lax.axis_size("line")
    areas = lax.axis_size("area")
    chips = owners // 2
    samples = traces.shape[1]
    panel = panels[0, 0]
    forward, forward_turns, inverse, turns = make_tables(samples, NF, owners)
    tables = (jnp.asarray(forward), jnp.asarray(forward_turns))
    inverse = jnp.asarray(inverse)
    turns = jnp.asarray(turns)

    line = lax.axis_index("line")
    chip, core = lax.shift_right_logical(line, 1), line & 1
    sign = 1 - 2 * core
    near = [(chip ^ d) * 2 + core for d in range(chips)]
    near_ids = jnp.stack(near + [sign, chip, core, lax.axis_index("area")]).astype(I32)
    all_ids = [(chip ^ (b // 2)) * 2 + (core ^ (b % 2)) for b in range(owners)]
    all_ids = jnp.stack(all_ids).astype(I32)

    panel_across = swap(panel, 1)
    traces_across = swap(traces, 1)
    facts = [panel_index, receiver_slot, owner.reshape(-1), aperture_weight]
    *near_panels, table, wide = near_of(near_ids, panel, *tables, facts)
    near_panels = send_blocks(near_panels)
    far_panels = forward_of(near_ids, [panel_across], table, wide, "far_panel_dft")
    far_panels = send_blocks(far_panels)
    spectra = forward_of(near_ids, [traces, traces_across], table, wide, "trace_dft")
    spectra = send_blocks(spectra)

    blocks = [block for pair in zip(near_panels, far_panels) for block in pair]
    main, edges, near_facts = choose(near_ids, plan, blocks)
    facts = [near_facts, swap(near_facts, 1)]
    border = lax.ppermute(edges, "area", [(i, i + 1) for i in range(areas - 1)])
    masks = masks_of(near_ids, facts, panel.shape[0], panel.shape[0] + EDGE)

    early = [0]
    late = [d for d in range(chips) if d not in early]
    partial = early_sums(early, main, border, masks, [spectra[d] for d in early])
    groups = []
    for first in range(0, STEPS, CHUNK):
        given = (main, border, partial, masks, [spectra[d] for d in late])
        sums = send_blocks(late_sums(first, chips, late, *given))
        across = swap(jnp.stack([block[1] for block in sums]), 1)
        groups.append(sums + [across])
    return inverse_of(all_ids, groups, inverse, turns)


def solution(mesh):
    in_specs = (
        P(("area", "line"), None),
        P(("area", "line"), None),
        P(("area", "line")),
        P(("area", "line")),
        P(("area", "line")),
        P("area", "line", None, None),
        P(),
    )
    out_specs = P(None, ("area", "line"), None)
    return jax.shard_map(local, mesh=mesh, in_specs=in_specs, out_specs=out_specs, check_vma=False)
```

```python
import functools
import math

import jax
import jax.numpy as jnp
import ml_dtypes
import numpy as np
from jax import lax
from jax.experimental import pallas as pl
from jax.experimental.pallas import tpu as pltpu
from jax.sharding import PartitionSpec as P

NF = 1024
EDGE = 64
STEPS = 4
RECV_DEV = 64
CHUNK = 2
BASE = 64
FACTS = 8
ROWS = 16
LANES = 128
F32 = jnp.float32
BF16 = jnp.bfloat16
I32 = jnp.int32


def vmem():
    return pl.BlockSpec(memory_space=pltpu.VMEM)


def hbm():
    return pl.BlockSpec(memory_space=pltpu.HBM)


def in_hbm(array):
    return pltpu.with_memory_space_constraint(array, pltpu.HBM)


def smem():
    return pl.BlockSpec(memory_space=pltpu.SMEM)


def params(mib):
    return pltpu.CompilerParams(vmem_limit_bytes=mib << 20)


@functools.lru_cache(maxsize=None)
def make_tables(samples, bins, owners):
    scaling = 1.0 / math.sqrt(samples)
    half, period, each = samples // 2, samples // owners, bins // owners
    ids = np.arange(half).reshape(1, half // period, period)
    ids = ids * np.arange(owners)[:, None, None] % samples
    forward_turns = ids * (2.0 * math.pi / samples)
    forward_turns = np.concatenate([np.cos(forward_turns), -np.sin(forward_turns)], 1)
    phases = np.outer(np.arange(each), np.arange(period)) % period * (2.0 * math.pi / period)
    real, imag = np.cos(phases) * scaling, np.sin(phases) * scaling
    inverse = np.concatenate(
        [np.concatenate([real, imag], 1), np.concatenate([-imag, real], 1)], 0
    )
    forward = inverse.T
    inverse = np.stack([inverse, 2.0 * inverse])
    inverse[0, 1:each] *= 2.0
    inverse[0, each + 1 :] *= 2.0
    phases = np.outer(np.arange(owners), np.arange(period)) * (2.0 * math.pi / samples)
    turns = np.stack([np.cos(phases), np.sin(phases)], 1).astype(np.float32)
    forward = np.ascontiguousarray(forward).astype(ml_dtypes.bfloat16)
    return forward, forward_turns.astype(np.float32), inverse.astype(ml_dtypes.bfloat16), turns


def facts_message(facts, height, cols):
    index, slot, owner, weight = [ref[...].astype(F32)[None, :] for ref in facts]
    high = index.astype(I32) // BASE
    first = weight.astype(BF16).astype(F32)
    second = (weight - first).astype(BF16).astype(F32)
    lines = [high.astype(F32), index - (high * BASE).astype(F32), slot, owner]
    lines += [first, second, weight - first - second, jnp.zeros_like(weight)]
    block = jnp.concatenate(lines, 0)
    parts = [block[:, at : at + cols] for at in range(0, block.shape[1], cols)]
    parts += [jnp.zeros((height - FACTS * len(parts), cols), F32)] * (height > FACTS * len(parts))
    return jnp.concatenate(parts, 0).astype(BF16)


def spread_turns(chips, ids_ref, turns_ref, wide_ref):
    for d in range(chips):
        turn = turns_ref[ids_ref[d]]
        for number in range(turn.shape[0]):
            wide_ref[d, number] = jnp.broadcast_to(turn[number : number + 1], wide_ref.shape[2:])


def turn_rows(ids_ref, x_ref, base, count, wide_ref, y_ref, at):
    chips, owners, _, period = wide_ref.shape
    half = owners // 2
    sign = ids_ref[chips].astype(F32)

    @pl.loop(0, count // ROWS)
    def _(chunk):
        row = pl.multiple_of(base + chunk * ROWS, ROWS)
        to = pl.multiple_of(at + chunk * ROWS, ROWS)
        for lane in range(0, period, LANES):
            stop = min(lane + LANES, period)
            folded = []
            for q in range(half):
                low = x_ref[pl.ds(row, ROWS), q * period + lane : q * period + stop]
                start = (q + half) * period
                high = x_ref[pl.ds(row, ROWS), start + lane : start + stop]
                folded.append(low.astype(F32) + high.astype(F32) * sign)
            for d in range(chips):
                for part in range(2):
                    total = folded[0] * wide_ref[d, part * half, :, lane:stop]
                    for q in range(1, half):
                        total += folded[q] * wide_ref[d, part * half + q, :, lane:stop]
                    start = part * period
                    y_ref[d, pl.ds(to, ROWS), start + lane : start + stop] = total.astype(BF16)


def first_kernel(chips, ids_ref, table_ref, turns_ref, x_ref, *refs):
    given, outs, (table, wide), refs = refs[:4], refs[4:][:chips], refs[4 + chips :][:2], refs[6 + chips :]
    turns, ready, taken, (y_ref, sems) = refs[0], refs[1], refs[2:6], refs[6:]
    rows = x_ref.shape[0]
    part = rows // 2
    pairs = [(turns_ref, turns)]
    pairs += [(x_ref.at[pl.ds(at, part)], ready.at[pl.ds(at, part)]) for at in (0, part)]
    pairs += [(table_ref, table), *zip(given, taken)]
    copies = [
        pltpu.make_async_copy(source, target, sems.at[i]) for i, (source, target) in enumerate(pairs)
    ]
    for copy in copies:
        copy.start()
    copies[0].wait()
    spread_turns(chips, ids_ref, turns, wide)
    for number in range(2):
        copies[1 + number].wait()
        turn_rows(ids_ref, ready, number * part, part, wide, y_ref, number * part)
    for copy in copies[3:]:
        copy.wait()
    message = facts_message(taken, outs[0].shape[0] - rows, outs[0].shape[1])
    for d in range(chips - 1, -1, -1):
        spectra = jnp.dot(y_ref[d], table[...], preferred_element_type=F32)
        outs[d][:rows, :] = spectra.astype(BF16)
        outs[d][rows:, :] = message


def cost_of(rows, table, turns):
    return pl.CostEstimate(
        flops=rows * turns.shape[0] * table.size,
        bytes_accessed=4 * rows * table.size // 64,
        transcendentals=0,
    )


def near_of(ids, panel, table, turns, facts):
    rows, samples = panel.shape
    cols = table.shape[1]
    chips = turns.shape[0] // 2
    owners, _, period = turns.shape
    height = 2 * FACTS * -(-rows // (2 * cols))
    return pl.pallas_call(
        functools.partial(first_kernel, chips),
        out_shape=[jax.ShapeDtypeStruct((rows + height, cols), BF16)] * chips
        + [
            jax.ShapeDtypeStruct(table.shape, BF16),
            jax.ShapeDtypeStruct((chips, owners, ROWS, period), F32),
        ],
        in_specs=[smem()] + [hbm()] * 7,
        out_specs=[vmem()] * (chips + 2),
        scratch_shapes=[pltpu.VMEM(turns.shape, F32), pltpu.VMEM((rows, samples), BF16)]
        + [pltpu.VMEM(fact.shape, fact.dtype) for fact in facts]
        + [pltpu.VMEM((chips, rows, 2 * period), BF16), pltpu.SemaphoreType.DMA((8,))],
        cost_estimate=cost_of(rows, table, turns),
        compiler_params=params(24),
        name="near_panel_dft",
    )(ids, *[in_hbm(array) for array in (table, turns, panel, *facts)])


def forward_kernel(chips, count, ids_ref, table_ref, wide, *refs):
    inputs, outs, y_ref = refs[:count], refs[count:-1], refs[-1]
    for number, x_ref in enumerate(inputs):
        rows = x_ref.shape[0]
        turn_rows(ids_ref, x_ref, 0, rows, wide, y_ref, number * rows)
    for d in range(chips - 1, -1, -1):
        outs[d][...] = jnp.dot(
            y_ref[d], table_ref[...], preferred_element_type=F32
        ).astype(BF16)


def forward_of(ids, arrays, table, wide, name):
    rows = len(arrays) * arrays[0].shape[0]
    cols = table.shape[1]
    chips, _, _, period = wide.shape
    count = len(arrays)
    return pl.pallas_call(
        functools.partial(forward_kernel, chips, count),
        out_shape=[jax.ShapeDtypeStruct((rows, cols), BF16)] * chips,
        in_specs=[smem()] + [vmem()] * (count + 2),
        out_specs=[vmem()] * chips,
        scratch_shapes=[pltpu.VMEM((chips, rows, 2 * period), BF16)],
        cost_estimate=cost_of(rows, table, wide),
        compiler_params=params(24),
        name=name,
    )(ids, table, wide, *arrays)


def masks_kernel(rows, ids_ref, *refs):
    facts, (gather_ref, summer_ref, weight_ref) = refs[:2], refs[2:]
    chips, height, cols = facts[0].shape
    chip, core = ids_ref[chips + 1], ids_ref[chips + 2]
    receivers = summer_ref.shape[0]
    extent = gather_ref.shape[1]
    square = (cols, cols)
    eye = (
        lax.broadcasted_iota(I32, square, 0) == lax.broadcasted_iota(I32, square, 1)
    ).astype(BF16)
    places = lax.broadcasted_iota(I32, (receivers, cols), 0)
    indices = lax.broadcasted_iota(I32, (cols, extent), 1)
    stacked = jnp.concatenate(
        [facts[across][distance] for distance in range(chips) for across in range(2)], 0
    )
    every = lax.dot_general(eye, stacked, (((1,), (1,)), ((), ())), preferred_element_type=F32)
    for distance in range(chips):
        for across in range(2):
            wide = facts[across][distance].astype(F32).astype(I32)
            where = 2 * distance + across
            turned = every[:, where * height : (where + 1) * height]
            for part in range(rows // cols):
                line = part * FACTS
                at = where * rows + part * cols
                slot, owner = wide[line + 2 : line + 3], wide[line + 3 : line + 4]
                place = (((owner >> 1) ^ chip) * 2 + ((owner & 1) ^ core)) * RECV_DEV + slot
                summer_ref[:, at : at + cols] = (places == place).astype(BF16)
                column = [turned[:, line + i : line + i + 1] for i in range(7)]
                index = (column[0] * BASE + column[1]).astype(I32)
                gather_ref[at : at + cols, :] = (indices == index).astype(BF16)
                weight = column[4] + column[5] + column[6]
                weight_ref[part * cols : (part + 1) * cols, where : where + 1] = weight


def masks_of(ids, facts, rows, extent):
    chips = facts[0].shape[0]
    traces = 2 * chips * rows
    receivers = 2 * chips * RECV_DEV
    return pl.pallas_call(
        functools.partial(masks_kernel, rows),
        out_shape=[
            jax.ShapeDtypeStruct((traces, extent), BF16),
            jax.ShapeDtypeStruct((receivers, traces), BF16),
            jax.ShapeDtypeStruct((rows, 2 * chips), F32),
        ],
        in_specs=[smem()] + [vmem()] * 2,
        out_specs=[vmem()] * 3,
        cost_estimate=pl.CostEstimate(
            flops=6 * traces * (extent + receivers),
            bytes_accessed=2 * traces * (extent + receivers),
            transcendentals=0,
        ),
        compiler_params=params(24),
        name="masks",
    )(ids, *facts)


def choose_kernel(rows, ids_ref, plan_ref, *refs):
    blocks, (main_ref, edges_ref, facts_ref) = refs[:-3], refs[-3:]
    chips = len(blocks) // 2
    for number in range(chips):
        facts_ref[number] = blocks[2 * number][rows:, :]
    for step in range(STEPS):
        planned = plan_ref[ids_ref[chips + 3], step]
        chosen = ((planned >> 1) ^ ids_ref[chips + 1]) * 2 + ((planned & 1) ^ ids_ref[chips + 2])
        for number, block in enumerate(blocks):

            @pl.when(chosen == number)
            def _():
                main_ref[step] = block[:rows, :]
                edges_ref[step] = block[rows - EDGE : rows, :]


def choose(ids, plan, blocks):
    rows, cols = blocks[1].shape
    height = blocks[0].shape[0] - rows
    return pl.pallas_call(
        functools.partial(choose_kernel, rows),
        out_shape=[
            jax.ShapeDtypeStruct((STEPS, rows, cols), BF16),
            jax.ShapeDtypeStruct((STEPS, EDGE, cols), BF16),
            jax.ShapeDtypeStruct((len(blocks) // 2, height, cols), BF16),
        ],
        in_specs=[smem(), smem()] + [vmem()] * len(blocks),
        out_specs=[vmem()] * 3,
        cost_estimate=pl.CostEstimate(
            flops=STEPS * rows * cols,
            bytes_accessed=2 * STEPS * rows * cols,
            transcendentals=0,
        ),
        compiler_params=params(24),
        name="choose_panels",
    )(ids, plan, *blocks)


def add_products(steps, distances, main_ref, border_ref, masks, spectra_refs, totals):
    gather_ref, summer_ref, weight_ref = masks
    half = main_ref.shape[2] // 2
    rows = weight_ref.shape[0]
    extended = [jnp.concatenate([main_ref[k], border_ref[k]], 0) for k in steps]
    for distance, spectra_ref in zip(distances, spectra_refs):
        for across in range(2):
            block = 2 * distance + across
            at = block * rows
            spectra = spectra_ref[across * rows : (across + 1) * rows, :].astype(F32)
            spectra = spectra * weight_ref[:, block : block + 1]
            real_d, imag_d = spectra[:, :half], spectra[:, half:]
            for number in range(len(steps)):
                picked = jnp.dot(
                    gather_ref[at : at + rows, :], extended[number], preferred_element_type=F32
                )
                real_p, imag_p = picked[:, :half], picked[:, half:]
                product = jnp.concatenate(
                    [real_p * real_d - imag_p * imag_d, real_p * imag_d + imag_p * real_d], 1
                ).astype(BF16)
                part = jnp.dot(
                    summer_ref[:, at : at + rows], product, preferred_element_type=F32
                )
                totals[number] = part if totals[number] is None else totals[number] + part
    return totals


def early_kernel(distances, main_ref, border_ref, *refs):
    masks, spectra_refs, partial_ref = refs[:3], refs[3:-1], refs[-1]
    for first in range(0, STEPS, CHUNK):
        steps = range(first, first + CHUNK)
        totals = [None] * CHUNK
        add_products(steps, distances, main_ref, border_ref, masks, spectra_refs, totals)
        for number, step in enumerate(steps):
            partial_ref[step] = totals[number]


def early_sums(distances, main, border, masks, spectra):
    cols = main.shape[2]
    gather, summer, _ = masks
    traces = len(spectra) * spectra[0].shape[0]
    return pl.pallas_call(
        functools.partial(early_kernel, distances),
        out_shape=jax.ShapeDtypeStruct((STEPS, summer.shape[0], cols), F32),
        in_specs=[vmem()] * (5 + len(spectra)),
        out_specs=vmem(),
        cost_estimate=pl.CostEstimate(
            flops=2 * STEPS * cols * traces * (gather.shape[1] + summer.shape[0]),
            bytes_accessed=2 * traces * cols,
            transcendentals=0,
        ),
        compiler_params=params(24),
        name="early_sums",
    )(main, border, *masks, *spectra)


def late_kernel(first, chips, distances, main_ref, border_ref, partial_ref, *refs):
    masks, spectra_refs, outs = refs[:3], refs[3:-chips], refs[-chips:]
    steps = range(first, first + CHUNK)
    totals = [partial_ref[step] for step in steps]
    add_products(steps, distances, main_ref, border_ref, masks, spectra_refs, totals)
    for number in range(CHUNK):
        result = totals[number].astype(BF16)
        for place in range(2 * chips):
            rows_of = result[place * RECV_DEV : (place + 1) * RECV_DEV]
            outs[place // 2][place % 2, number] = rows_of


def late_sums(first, chips, distances, main, border, partial, masks, spectra):
    cols = main.shape[2]
    gather, summer, _ = masks
    traces = len(spectra) * spectra[0].shape[0]
    return pl.pallas_call(
        functools.partial(late_kernel, first, chips, distances),
        out_shape=[jax.ShapeDtypeStruct((2, CHUNK, RECV_DEV, cols), BF16)] * chips,
        in_specs=[vmem()] * (6 + len(spectra)),
        out_specs=[vmem()] * chips,
        cost_estimate=pl.CostEstimate(
            flops=2 * CHUNK * cols * traces * (gather.shape[1] + summer.shape[0]),
            bytes_accessed=2 * traces * cols,
            transcendentals=0,
        ),
        compiler_params=params(24),
        name="receiver_sums",
    )(main, border, partial, *masks, *spectra)


def weighted_sum(terms):
    by_size = {}
    for coefficient, term in terms:
        size = round(abs(coefficient), 12)
        if size == 0.0:
            continue
        before = by_size.get(size)
        if before is None:
            by_size[size] = (term, coefficient)
        elif (before[1] < 0) == (coefficient < 0):
            by_size[size] = (before[0] + term, before[1])
        else:
            by_size[size] = (before[0] - term, before[1])
    total = None
    for term, coefficient in by_size.values():
        if abs(abs(coefficient) - 1.0) > 1e-9:
            term = term * coefficient
        elif coefficient < 0:
            term = -term
        total = term if total is None else total + term
    return total


def inverse_kernel(chips, first, ids_ref, table_ref, turns_ref, *refs):
    group = refs[: chips + 1]
    out_ref, real_ref, imag_ref, sems = refs[-4 - CHUNK : -1 - CHUNK] + refs[-1:]
    ready = refs[-1 - CHUNK : -1]
    owners, _, period = turns_ref.shape
    cols = table_ref.shape[1]
    for distance in range(chips):
        for across in range(2):
            part = group[distance][0] if across == 0 else group[chips][distance]
            line = ids_ref[2 * distance + across]
            spread = jnp.dot(
                part.reshape(CHUNK * RECV_DEV, cols),
                table_ref[jnp.minimum(line, 1)],
                preferred_element_type=F32,
            )
            real, imag = spread[:, :period], spread[:, period:]
            turn = turns_ref[line]
            real_ref[line] = real * turn[0:1] - imag * turn[1:2]
            imag_ref[line] = real * turn[1:2] + imag * turn[0:1]

    angles = [[2.0 * math.pi * (r * q % owners) / owners for r in range(owners)] for q in range(owners)]

    def add_up(step, chunk):
        row = pl.multiple_of(chunk * ROWS, ROWS)
        at = pl.multiple_of(step * RECV_DEV + chunk * ROWS, ROWS)
        for lane in range(0, period, LANES):
            lanes = slice(lane, min(lane + LANES, period))
            real = [real_ref[r, pl.ds(at, ROWS), lanes] for r in range(owners)]
            imag = [imag_ref[r, pl.ds(at, ROWS), lanes] for r in range(owners)]
            for q in range(owners // 2):
                sums = []
                for parity in range(2):
                    terms = []
                    for r in range(parity, owners, 2):
                        terms += [(math.cos(angles[q][r]), real[r])]
                        terms += [(-math.sin(angles[q][r]), imag[r])]
                    sums.append(weighted_sum(terms))
                for value, place in ((sums[0] + sums[1], q), (sums[0] - sums[1], q + owners // 2)):
                    start = place * period + lane
                    ready[step][pl.ds(row, ROWS), start : start + lanes.stop - lane] = (
                        value.astype(BF16)
                    )

    copies = [
        pltpu.make_async_copy(ready[step], out_ref.at[first + step], sems.at[step])
        for step in range(CHUNK)
    ]
    for step in range(CHUNK):
        pl.loop(0, RECV_DEV // ROWS)(functools.partial(add_up, step))
        copies[step].start()
    for copy in copies:
        copy.wait()


def inverse_of(ids, first, group, table, turns, before):
    owners, _, period = turns.shape
    rows, samples = CHUNK * RECV_DEV, owners * period
    given, aliases = [*group], {}
    specs = [smem()] + [vmem()] * (2 + len(group))
    if before is not None:
        aliases = {len(specs): 0}
        given, specs = given + [before], specs + [hbm()]
    return pl.pallas_call(
        functools.partial(inverse_kernel, owners // 2, first),
        in_specs=specs,
        out_specs=hbm(),
        out_shape=jax.ShapeDtypeStruct((STEPS, RECV_DEV, samples), BF16),
        scratch_shapes=[pltpu.VMEM((owners, rows, period), F32)] * 2
        + [pltpu.VMEM((RECV_DEV, samples), BF16)] * CHUNK
        + [pltpu.SemaphoreType.DMA((CHUNK,))],
        input_output_aliases=aliases,
        cost_estimate=pl.CostEstimate(
            flops=2 * rows * owners * table[0].size,
            bytes_accessed=2 * rows * owners * period,
            transcendentals=0,
        ),
        compiler_params=params(24),
        name="inverse_dft",
    )(ids, table, turns, *given)


def swap(array, distance):
    devices = range(lax.axis_size("line"))
    return lax.ppermute(array, "line", [(i, i ^ distance) for i in devices])


def send_blocks(blocks):
    chips = len(blocks)
    sent = {d: swap(blocks[d], 2 * d) for d in range(chips - 1, 0, -1)}
    return [blocks[0]] + [sent[d] for d in range(1, chips)]


def local(traces, owner, panel_index, receiver_slot, aperture_weight, panels, plan):
    owners = lax.axis_size("line")
    areas = lax.axis_size("area")
    chips = owners // 2
    samples = traces.shape[1]
    panel = panels[0, 0]
    forward, forward_turns, inverse, turns = make_tables(samples, NF, owners)
    tables = (jnp.asarray(forward), jnp.asarray(forward_turns))
    inverse = jnp.asarray(inverse)
    turns = jnp.asarray(turns)

    line = lax.axis_index("line")
    chip, core = lax.shift_right_logical(line, 1), line & 1
    sign = 1 - 2 * core
    near = [(chip ^ d) * 2 + core for d in range(chips)]
    near_ids = jnp.stack(near + [sign, chip, core, lax.axis_index("area")]).astype(I32)
    all_ids = [(chip ^ (b // 2)) * 2 + (core ^ (b % 2)) for b in range(owners)]
    all_ids = jnp.stack(all_ids).astype(I32)

    panel_across = swap(panel, 1)
    traces_across = swap(traces, 1)
    facts = [panel_index, receiver_slot, owner.reshape(-1), aperture_weight]
    *near_panels, table, wide = near_of(near_ids, panel, *tables, facts)
    near_panels = send_blocks(near_panels)
    far_panels = forward_of(near_ids, [panel_across], table, wide, "far_panel_dft")
    far_panels = send_blocks(far_panels)
    spectra = forward_of(near_ids, [traces, traces_across], table, wide, "trace_dft")
    spectra = send_blocks(spectra)

    blocks = [block for pair in zip(near_panels, far_panels) for block in pair]
    main, edges, near_facts = choose(near_ids, plan, blocks)
    facts = [near_facts, swap(near_facts, 1)]
    border = lax.ppermute(edges, "area", [(i, i + 1) for i in range(areas - 1)])
    masks = masks_of(near_ids, facts, panel.shape[0], panel.shape[0] + EDGE)

    early = [0]
    late = [d for d in range(chips) if d not in early]
    partial = early_sums(early, main, border, masks, [spectra[d] for d in early])
    result = None
    for first in range(0, STEPS, CHUNK):
        given = (main, border, partial, masks, [spectra[d] for d in late])
        sums = send_blocks(late_sums(first, chips, late, *given))
        across = swap(jnp.stack([block[1] for block in sums]), 1)
        result = inverse_of(all_ids, first, sums + [across], inverse, turns, result)
    return result


def solution(mesh):
    in_specs = (
        P(("area", "line"), None),
        P(("area", "line"), None),
        P(("area", "line")),
        P(("area", "line")),
        P(("area", "line")),
        P("area", "line", None, None),
        P(),
    )
    out_specs = P(None, ("area", "line"), None)
    return jax.shard_map(local, mesh=mesh, in_specs=in_specs, out_specs=out_specs, check_vma=False)
```

```python
import functools
import math

import jax
import jax.numpy as jnp
import ml_dtypes
import numpy as np
from jax import lax
from jax.experimental import pallas as pl
from jax.experimental.pallas import tpu as pltpu
from jax.sharding import PartitionSpec as P

NF = 1024
EDGE = 64
STEPS = 4
RECV_DEV = 64
CHUNK = 2
BASE = 64
FACTS = 8
ROWS = 16
LANES = 128
F32 = jnp.float32
BF16 = jnp.bfloat16
I32 = jnp.int32


def vmem():
    return pl.BlockSpec(memory_space=pltpu.VMEM)


def hbm():
    return pl.BlockSpec(memory_space=pltpu.HBM)


def in_hbm(array):
    return pltpu.with_memory_space_constraint(array, pltpu.HBM)


def smem():
    return pl.BlockSpec(memory_space=pltpu.SMEM)


def params(mib):
    return pltpu.CompilerParams(vmem_limit_bytes=mib << 20)


@functools.lru_cache(maxsize=None)
def make_tables(samples, bins, owners):
    scaling = 1.0 / math.sqrt(samples)
    half, period, each = samples // 2, samples // owners, bins // owners
    ids = np.arange(half).reshape(1, half // period, period)
    ids = ids * np.arange(owners)[:, None, None] % samples
    forward_turns = ids * (2.0 * math.pi / samples)
    forward_turns = np.concatenate([np.cos(forward_turns), -np.sin(forward_turns)], 1)
    phases = np.outer(np.arange(each), np.arange(period)) % period * (2.0 * math.pi / period)
    real, imag = np.cos(phases) * scaling, np.sin(phases) * scaling
    inverse = np.concatenate(
        [np.concatenate([real, imag], 1), np.concatenate([-imag, real], 1)], 0
    )
    forward = inverse.T
    inverse = np.stack([inverse, 2.0 * inverse])
    inverse[0, 1:each] *= 2.0
    inverse[0, each + 1 :] *= 2.0
    phases = np.outer(np.arange(owners), np.arange(period)) * (2.0 * math.pi / samples)
    turns = np.stack([np.cos(phases), np.sin(phases)], 1).astype(np.float32)
    forward = np.ascontiguousarray(forward).astype(ml_dtypes.bfloat16)
    return forward, forward_turns.astype(np.float32), inverse.astype(ml_dtypes.bfloat16), turns


def facts_message(facts, height, cols):
    index, slot, owner, weight = [ref[...].astype(F32)[None, :] for ref in facts]
    high = index.astype(I32) // BASE
    first = weight.astype(BF16).astype(F32)
    second = (weight - first).astype(BF16).astype(F32)
    lines = [high.astype(F32), index - (high * BASE).astype(F32), slot, owner]
    lines += [first, second, weight - first - second, jnp.zeros_like(weight)]
    block = jnp.concatenate(lines, 0)
    parts = [block[:, at : at + cols] for at in range(0, block.shape[1], cols)]
    parts += [jnp.zeros((height - FACTS * len(parts), cols), F32)] * (height > FACTS * len(parts))
    return jnp.concatenate(parts, 0).astype(BF16)


def spread_turns(chips, ids_ref, turns_ref, wide_ref):
    for d in range(chips):
        turn = turns_ref[ids_ref[d]]
        for number in range(turn.shape[0]):
            wide_ref[d, number] = jnp.broadcast_to(turn[number : number + 1], wide_ref.shape[2:])


def turn_rows(ids_ref, x_ref, base, count, wide_ref, y_ref, at):
    chips, owners, _, period = wide_ref.shape
    half = owners // 2
    sign = ids_ref[chips].astype(F32)

    @pl.loop(0, count // ROWS, unroll=8)
    def _(chunk):
        row = pl.multiple_of(base + chunk * ROWS, ROWS)
        to = pl.multiple_of(at + chunk * ROWS, ROWS)
        for lane in range(0, period, LANES):
            stop = min(lane + LANES, period)
            folded = []
            for q in range(half):
                low = x_ref[pl.ds(row, ROWS), q * period + lane : q * period + stop]
                start = (q + half) * period
                high = x_ref[pl.ds(row, ROWS), start + lane : start + stop]
                folded.append(low.astype(F32) + high.astype(F32) * sign)
            for d in range(chips):
                for part in range(2):
                    total = folded[0] * wide_ref[d, part * half, :, lane:stop]
                    for q in range(1, half):
                        total += folded[q] * wide_ref[d, part * half + q, :, lane:stop]
                    start = part * period
                    y_ref[d, pl.ds(to, ROWS), start + lane : start + stop] = total.astype(BF16)


def first_kernel(chips, ids_ref, table_ref, turns_ref, x_ref, *refs):
    given, outs, (table, wide), refs = refs[:4], refs[4:][:chips], refs[4 + chips :][:2], refs[6 + chips :]
    turns, ready, taken, (y_ref, sems) = refs[0], refs[1], refs[2:6], refs[6:]
    rows = x_ref.shape[0]
    part = rows // 2
    pairs = [(turns_ref, turns)]
    pairs += [(x_ref.at[pl.ds(at, part)], ready.at[pl.ds(at, part)]) for at in (0, part)]
    pairs += [(table_ref, table), *zip(given, taken)]
    copies = [
        pltpu.make_async_copy(source, target, sems.at[i]) for i, (source, target) in enumerate(pairs)
    ]
    for copy in copies:
        copy.start()
    copies[0].wait()
    spread_turns(chips, ids_ref, turns, wide)
    for number in range(2):
        copies[1 + number].wait()
        turn_rows(ids_ref, ready, number * part, part, wide, y_ref, number * part)
    for copy in copies[3:]:
        copy.wait()
    message = facts_message(taken, outs[0].shape[0] - rows, outs[0].shape[1])
    for d in range(chips - 1, -1, -1):
        spectra = jnp.dot(y_ref[d], table[...], preferred_element_type=F32)
        outs[d][:rows, :] = spectra.astype(BF16)
        outs[d][rows:, :] = message


def cost_of(rows, table, turns):
    return pl.CostEstimate(
        flops=rows * turns.shape[0] * table.size,
        bytes_accessed=4 * rows * table.size // 64,
        transcendentals=0,
    )


def near_of(ids, panel, table, turns, facts):
    rows, samples = panel.shape
    cols = table.shape[1]
    chips = turns.shape[0] // 2
    owners, _, period = turns.shape
    height = 2 * FACTS * -(-rows // (2 * cols))
    return pl.pallas_call(
        functools.partial(first_kernel, chips),
        out_shape=[jax.ShapeDtypeStruct((rows + height, cols), BF16)] * chips
        + [
            jax.ShapeDtypeStruct(table.shape, BF16),
            jax.ShapeDtypeStruct((chips, owners, ROWS, period), F32),
        ],
        in_specs=[smem()] + [hbm()] * 7,
        out_specs=[vmem()] * (chips + 2),
        scratch_shapes=[pltpu.VMEM(turns.shape, F32), pltpu.VMEM((rows, samples), BF16)]
        + [pltpu.VMEM(fact.shape, fact.dtype) for fact in facts]
        + [pltpu.VMEM((chips, rows, 2 * period), BF16), pltpu.SemaphoreType.DMA((8,))],
        cost_estimate=cost_of(rows, table, turns),
        compiler_params=params(24),
        name="near_panel_dft",
    )(ids, *[in_hbm(array) for array in (table, turns, panel, *facts)])


def forward_kernel(chips, count, ids_ref, table_ref, wide, *refs):
    inputs, outs, y_ref = refs[:count], refs[count:-1], refs[-1]
    for number, x_ref in enumerate(inputs):
        rows = x_ref.shape[0]
        turn_rows(ids_ref, x_ref, 0, rows, wide, y_ref, number * rows)
    for d in range(chips - 1, -1, -1):
        outs[d][...] = jnp.dot(
            y_ref[d], table_ref[...], preferred_element_type=F32
        ).astype(BF16)


def forward_of(ids, arrays, table, wide, name):
    rows = len(arrays) * arrays[0].shape[0]
    cols = table.shape[1]
    chips, _, _, period = wide.shape
    count = len(arrays)
    return pl.pallas_call(
        functools.partial(forward_kernel, chips, count),
        out_shape=[jax.ShapeDtypeStruct((rows, cols), BF16)] * chips,
        in_specs=[smem()] + [vmem()] * (count + 2),
        out_specs=[vmem()] * chips,
        scratch_shapes=[pltpu.VMEM((chips, rows, 2 * period), BF16)],
        cost_estimate=cost_of(rows, table, wide),
        compiler_params=params(24),
        name=name,
    )(ids, table, wide, *arrays)


def masks_kernel(rows, ids_ref, *refs):
    facts, (gather_ref, summer_ref, weight_ref) = refs[:2], refs[2:]
    chips, height, cols = facts[0].shape
    chip, core = ids_ref[chips + 1], ids_ref[chips + 2]
    receivers = summer_ref.shape[0]
    extent = gather_ref.shape[1]
    square = (cols, cols)
    eye = (
        lax.broadcasted_iota(I32, square, 0) == lax.broadcasted_iota(I32, square, 1)
    ).astype(BF16)
    places = lax.broadcasted_iota(I32, (receivers, cols), 0)
    indices = lax.broadcasted_iota(I32, (cols, extent), 1)
    stacked = jnp.concatenate(
        [facts[across][distance] for distance in range(chips) for across in range(2)], 0
    )
    every = lax.dot_general(eye, stacked, (((1,), (1,)), ((), ())), preferred_element_type=F32)
    for distance in range(chips):
        for across in range(2):
            wide = facts[across][distance].astype(F32).astype(I32)
            where = 2 * distance + across
            turned = every[:, where * height : (where + 1) * height]
            for part in range(rows // cols):
                line = part * FACTS
                at = where * rows + part * cols
                slot, owner = wide[line + 2 : line + 3], wide[line + 3 : line + 4]
                place = (((owner >> 1) ^ chip) * 2 + ((owner & 1) ^ core)) * RECV_DEV + slot
                summer_ref[:, at : at + cols] = (places == place).astype(BF16)
                column = [turned[:, line + i : line + i + 1] for i in range(7)]
                index = (column[0] * BASE + column[1]).astype(I32)
                gather_ref[at : at + cols, :] = (indices == index).astype(BF16)
                weight = column[4] + column[5] + column[6]
                weight_ref[part * cols : (part + 1) * cols, where : where + 1] = weight


def masks_of(ids, facts, rows, extent):
    chips = facts[0].shape[0]
    traces = 2 * chips * rows
    receivers = 2 * chips * RECV_DEV
    return pl.pallas_call(
        functools.partial(masks_kernel, rows),
        out_shape=[
            jax.ShapeDtypeStruct((traces, extent), BF16),
            jax.ShapeDtypeStruct((receivers, traces), BF16),
            jax.ShapeDtypeStruct((rows, 2 * chips), F32),
        ],
        in_specs=[smem()] + [vmem()] * 2,
        out_specs=[vmem()] * 3,
        cost_estimate=pl.CostEstimate(
            flops=6 * traces * (extent + receivers),
            bytes_accessed=2 * traces * (extent + receivers),
            transcendentals=0,
        ),
        compiler_params=params(24),
        name="masks",
    )(ids, *facts)


def choose_kernel(rows, ids_ref, plan_ref, *refs):
    blocks, (main_ref, edges_ref, facts_ref) = refs[:-3], refs[-3:]
    chips = len(blocks) // 2
    for number in range(chips):
        facts_ref[number] = blocks[2 * number][rows:, :]
    for step in range(STEPS):
        planned = plan_ref[ids_ref[chips + 3], step]
        chosen = ((planned >> 1) ^ ids_ref[chips + 1]) * 2 + ((planned & 1) ^ ids_ref[chips + 2])
        for number, block in enumerate(blocks):

            @pl.when(chosen == number)
            def _():
                main_ref[step] = block[:rows, :]
                edges_ref[step] = block[rows - EDGE : rows, :]


def choose(ids, plan, blocks):
    rows, cols = blocks[1].shape
    height = blocks[0].shape[0] - rows
    return pl.pallas_call(
        functools.partial(choose_kernel, rows),
        out_shape=[
            jax.ShapeDtypeStruct((STEPS, rows, cols), BF16),
            jax.ShapeDtypeStruct((STEPS, EDGE, cols), BF16),
            jax.ShapeDtypeStruct((len(blocks) // 2, height, cols), BF16),
        ],
        in_specs=[smem(), smem()] + [vmem()] * len(blocks),
        out_specs=[vmem()] * 3,
        cost_estimate=pl.CostEstimate(
            flops=STEPS * rows * cols,
            bytes_accessed=2 * STEPS * rows * cols,
            transcendentals=0,
        ),
        compiler_params=params(24),
        name="choose_panels",
    )(ids, plan, *blocks)


def add_products(steps, distances, main_ref, border_ref, masks, spectra_refs, totals):
    gather_ref, summer_ref, weight_ref = masks
    half = main_ref.shape[2] // 2
    rows = weight_ref.shape[0]
    extended = [jnp.concatenate([main_ref[k], border_ref[k]], 0) for k in steps]
    for distance, spectra_ref in zip(distances, spectra_refs):
        for across in range(2):
            block = 2 * distance + across
            at = block * rows
            spectra = spectra_ref[across * rows : (across + 1) * rows, :].astype(F32)
            spectra = spectra * weight_ref[:, block : block + 1]
            real_d, imag_d = spectra[:, :half], spectra[:, half:]
            for number in range(len(steps)):
                picked = jnp.dot(
                    gather_ref[at : at + rows, :], extended[number], preferred_element_type=F32
                )
                real_p, imag_p = picked[:, :half], picked[:, half:]
                product = jnp.concatenate(
                    [real_p * real_d - imag_p * imag_d, real_p * imag_d + imag_p * real_d], 1
                ).astype(BF16)
                part = jnp.dot(
                    summer_ref[:, at : at + rows], product, preferred_element_type=F32
                )
                totals[number] = part if totals[number] is None else totals[number] + part
    return totals


def early_kernel(distances, main_ref, border_ref, *refs):
    masks, spectra_refs, partial_ref = refs[:3], refs[3:-1], refs[-1]
    for first in range(0, STEPS, CHUNK):
        steps = range(first, first + CHUNK)
        totals = [None] * CHUNK
        add_products(steps, distances, main_ref, border_ref, masks, spectra_refs, totals)
        for number, step in enumerate(steps):
            partial_ref[step] = totals[number]


def early_sums(distances, main, border, masks, spectra):
    cols = main.shape[2]
    gather, summer, _ = masks
    traces = len(spectra) * spectra[0].shape[0]
    return pl.pallas_call(
        functools.partial(early_kernel, distances),
        out_shape=jax.ShapeDtypeStruct((STEPS, summer.shape[0], cols), F32),
        in_specs=[vmem()] * (5 + len(spectra)),
        out_specs=vmem(),
        cost_estimate=pl.CostEstimate(
            flops=2 * STEPS * cols * traces * (gather.shape[1] + summer.shape[0]),
            bytes_accessed=2 * traces * cols,
            transcendentals=0,
        ),
        compiler_params=params(24),
        name="early_sums",
    )(main, border, *masks, *spectra)


def late_kernel(first, chips, distances, main_ref, border_ref, partial_ref, *refs):
    masks, spectra_refs, outs = refs[:3], refs[3:-chips], refs[-chips:]
    steps = range(first, first + CHUNK)
    totals = [partial_ref[step] for step in steps]
    add_products(steps, distances, main_ref, border_ref, masks, spectra_refs, totals)
    for number in range(CHUNK):
        result = totals[number].astype(BF16)
        for place in range(2 * chips):
            rows_of = result[place * RECV_DEV : (place + 1) * RECV_DEV]
            outs[place // 2][place % 2, number] = rows_of


def late_sums(first, chips, distances, main, border, partial, masks, spectra):
    cols = main.shape[2]
    gather, summer, _ = masks
    traces = len(spectra) * spectra[0].shape[0]
    return pl.pallas_call(
        functools.partial(late_kernel, first, chips, distances),
        out_shape=[jax.ShapeDtypeStruct((2, CHUNK, RECV_DEV, cols), BF16)] * chips,
        in_specs=[vmem()] * (6 + len(spectra)),
        out_specs=[vmem()] * chips,
        cost_estimate=pl.CostEstimate(
            flops=2 * CHUNK * cols * traces * (gather.shape[1] + summer.shape[0]),
            bytes_accessed=2 * traces * cols,
            transcendentals=0,
        ),
        compiler_params=params(24),
        name="receiver_sums",
    )(main, border, partial, *masks, *spectra)


def weighted_sum(terms):
    by_size = {}
    for coefficient, term in terms:
        size = round(abs(coefficient), 12)
        if size == 0.0:
            continue
        before = by_size.get(size)
        if before is None:
            by_size[size] = (term, coefficient)
        elif (before[1] < 0) == (coefficient < 0):
            by_size[size] = (before[0] + term, before[1])
        else:
            by_size[size] = (before[0] - term, before[1])
    total = None
    for term, coefficient in by_size.values():
        if abs(abs(coefficient) - 1.0) > 1e-9:
            term = term * coefficient
        elif coefficient < 0:
            term = -term
        total = term if total is None else total + term
    return total


def inverse_kernel(chips, first, ids_ref, table_ref, turns_ref, *refs):
    group = refs[: chips + 1]
    out_ref, real_ref, imag_ref, sems = refs[-4 - CHUNK : -1 - CHUNK] + refs[-1:]
    ready = refs[-1 - CHUNK : -1]
    owners, _, period = turns_ref.shape
    cols = table_ref.shape[1]
    for distance in range(chips):
        for across in range(2):
            part = group[distance][0] if across == 0 else group[chips][distance]
            line = ids_ref[2 * distance + across]
            spread = jnp.dot(
                part.reshape(CHUNK * RECV_DEV, cols),
                table_ref[jnp.minimum(line, 1)],
                preferred_element_type=F32,
            )
            real, imag = spread[:, :period], spread[:, period:]
            turn = turns_ref[line]
            real_ref[line] = real * turn[0:1] - imag * turn[1:2]
            imag_ref[line] = real * turn[1:2] + imag * turn[0:1]

    angles = [[2.0 * math.pi * (r * q % owners) / owners for r in range(owners)] for q in range(owners)]

    def add_up(step, chunk):
        row = pl.multiple_of(chunk * ROWS, ROWS)
        at = pl.multiple_of(step * RECV_DEV + chunk * ROWS, ROWS)
        for lane in range(0, period, LANES):
            lanes = slice(lane, min(lane + LANES, period))
            real = [real_ref[r, pl.ds(at, ROWS), lanes] for r in range(owners)]
            imag = [imag_ref[r, pl.ds(at, ROWS), lanes] for r in range(owners)]
            for q in range(owners // 2):
                sums = []
                for parity in range(2):
                    terms = []
                    for r in range(parity, owners, 2):
                        terms += [(math.cos(angles[q][r]), real[r])]
                        terms += [(-math.sin(angles[q][r]), imag[r])]
                    sums.append(weighted_sum(terms))
                for value, place in ((sums[0] + sums[1], q), (sums[0] - sums[1], q + owners // 2)):
                    start = place * period + lane
                    ready[step][pl.ds(row, ROWS), start : start + lanes.stop - lane] = (
                        value.astype(BF16)
                    )

    copies = [
        pltpu.make_async_copy(ready[step], out_ref.at[first + step], sems.at[step])
        for step in range(CHUNK)
    ]
    for step in range(CHUNK):
        pl.loop(0, RECV_DEV // ROWS, unroll=4)(functools.partial(add_up, step))
        copies[step].start()
    for copy in copies:
        copy.wait()


def inverse_of(ids, first, group, table, turns, before):
    owners, _, period = turns.shape
    rows, samples = CHUNK * RECV_DEV, owners * period
    given, aliases = [*group], {}
    specs = [smem()] + [vmem()] * (2 + len(group))
    if before is not None:
        aliases = {len(specs): 0}
        given, specs = given + [before], specs + [hbm()]
    return pl.pallas_call(
        functools.partial(inverse_kernel, owners // 2, first),
        in_specs=specs,
        out_specs=hbm(),
        out_shape=jax.ShapeDtypeStruct((STEPS, RECV_DEV, samples), BF16),
        scratch_shapes=[pltpu.VMEM((owners, rows, period), F32)] * 2
        + [pltpu.VMEM((RECV_DEV, samples), BF16)] * CHUNK
        + [pltpu.SemaphoreType.DMA((CHUNK,))],
        input_output_aliases=aliases,
        cost_estimate=pl.CostEstimate(
            flops=2 * rows * owners * table[0].size,
            bytes_accessed=2 * rows * owners * period,
            transcendentals=0,
        ),
        compiler_params=params(24),
        name="inverse_dft",
    )(ids, table, turns, *given)


def swap(array, distance):
    devices = range(lax.axis_size("line"))
    return lax.ppermute(array, "line", [(i, i ^ distance) for i in devices])


def send_blocks(blocks):
    chips = len(blocks)
    sent = {d: swap(blocks[d], 2 * d) for d in range(chips - 1, 0, -1)}
    return [blocks[0]] + [sent[d] for d in range(1, chips)]


def local(traces, owner, panel_index, receiver_slot, aperture_weight, panels, plan):
    owners = lax.axis_size("line")
    areas = lax.axis_size("area")
    chips = owners // 2
    samples = traces.shape[1]
    panel = panels[0, 0]
    forward, forward_turns, inverse, turns = make_tables(samples, NF, owners)
    tables = (jnp.asarray(forward), jnp.asarray(forward_turns))
    inverse = jnp.asarray(inverse)
    turns = jnp.asarray(turns)

    line = lax.axis_index("line")
    chip, core = lax.shift_right_logical(line, 1), line & 1
    sign = 1 - 2 * core
    near = [(chip ^ d) * 2 + core for d in range(chips)]
    near_ids = jnp.stack(near + [sign, chip, core, lax.axis_index("area")]).astype(I32)
    all_ids = [(chip ^ (b // 2)) * 2 + (core ^ (b % 2)) for b in range(owners)]
    all_ids = jnp.stack(all_ids).astype(I32)

    panel_across = swap(panel, 1)
    traces_across = swap(traces, 1)
    facts = [panel_index, receiver_slot, owner.reshape(-1), aperture_weight]
    *near_panels, table, wide = near_of(near_ids, panel, *tables, facts)
    near_panels = send_blocks(near_panels)
    far_panels = forward_of(near_ids, [panel_across], table, wide, "far_panel_dft")
    far_panels = send_blocks(far_panels)
    spectra = forward_of(near_ids, [traces, traces_across], table, wide, "trace_dft")
    spectra = send_blocks(spectra)

    blocks = [block for pair in zip(near_panels, far_panels) for block in pair]
    main, edges, near_facts = choose(near_ids, plan, blocks)
    facts = [near_facts, swap(near_facts, 1)]
    border = lax.ppermute(edges, "area", [(i, i + 1) for i in range(areas - 1)])
    masks = masks_of(near_ids, facts, panel.shape[0], panel.shape[0] + EDGE)

    early = [0]
    late = [d for d in range(chips) if d not in early]
    partial = early_sums(early, main, border, masks, [spectra[d] for d in early])
    result = None
    for first in range(0, STEPS, CHUNK):
        given = (main, border, partial, masks, [spectra[d] for d in late])
        sums = send_blocks(late_sums(first, chips, late, *given))
        across = swap(jnp.stack([block[1] for block in sums]), 1)
        result = inverse_of(all_ids, first, sums + [across], inverse, turns, result)
    return result


def solution(mesh):
    in_specs = (
        P(("area", "line"), None),
        P(("area", "line"), None),
        P(("area", "line")),
        P(("area", "line")),
        P(("area", "line")),
        P("area", "line", None, None),
        P(),
    )
    out_specs = P(None, ("area", "line"), None)
    return jax.shard_map(local, mesh=mesh, in_specs=in_specs, out_specs=out_specs, check_vma=False)
```
